128 devices in a mesh: clus: 16 (over y, x), leaf: 8 (over z, core).
Axes of the slice: x: 4, y: 4, z: 4, core: 2. Of those that a mesh axis runs over, the one named last changes fastest.
Arguments:
- right_sides: bfloat16 [32, 8, 98304], P(None, 'leaf', 'clus'), may hold values from -6 to 6
- near_blocks: bfloat16 [8, 384, 5, 256, 256], P('leaf', 'clus'), may hold values from -0.15625 to 0.15625
- near_cols: int32 [8, 384, 5], P('leaf', 'clus'), may hold values from 0 to 383, as said below
- near_count: int32 [8, 384], P('leaf', 'clus'), may hold values from 1 to 5, as said below
- basis: bfloat16 [8, 384, 256, 64], P('leaf', 'clus'), may hold values from -0.375 to 0.375
- leaf_transfer: bfloat16 [8, 384, 64, 64], P('leaf', 'clus'), may hold values from -0.75 to 0.75
- par_transfer: bfloat16 [8, 96, 64, 64], P('leaf', 'clus'), may hold values from -0.75 to 0.75
- leaf_src: int32 [8, 384, 8], P('leaf', 'clus'), may hold values from 0 to 383, as said below
- leaf_coup: bfloat16 [8, 384, 8, 64, 64], P('leaf', 'clus'), may hold values from -0.25 to 0.25
- par_src: int32 [8, 96, 27], P('leaf', 'clus'), may hold values from 0 to 767, as said below
- par_coup: bfloat16 [8, 96, 27, 64, 64], P('leaf', 'clus'), may hold values from -0.15625 to 0.15625
- top_src: int32 [8, 16, 27], P('leaf', 'clus'), may hold values from 0 to 127
- top_coup: bfloat16 [8, 16, 27, 64, 64], P('leaf', 'clus'), may hold values from -0.15625 to 0.15625
Outputs:
- product: bfloat16 [32, 8, 98304], P(None, 'leaf', 'clus')
The draws below stay inside these ranges and needn't reach their ends.
Inputs may be any that keep to these rules, and one draw needn't show every extreme that they name: near_cols[s, g, 0] is g; the other slots name leaves within 8 of g in the same subtree. `near_count`: each subtree has a leaf with all 5 slots used. `leaf_src`: each entry names a leaf other than g within 8 of g in the same subtree. `par_src`: parent q is parent q % 96 of subtree q // 96; among the 162 entries of the parents of one device, at most 3 name parents held by one device, and some device is named exactly 3 times.
All inputs are finite; a program needn't handle non-finite values.
Results may differ from the reference program's by a relative error of at most 0.015.
Values may be sent and summed in bfloat16 or wider, within the bound.
A program may use at most 128 MiB of HBM per device.

```python
import jax
import jax.numpy as jnp
from jax import lax

B = 256
K = 64
R = 32
NEAR = 5
COUP0 = 8
COUP1 = 27
COUP2 = 27
REACH = 8
PAR_DEV = 6
SUBTREES = 8
LEAVES = 384
PARENTS = 96
TOPS = 128
PTS = 98304
N_CLUS = 16


def window_partners(key, wanted):
    shape = (SUBTREES, LEAVES, 2 * REACH)
    scores = jax.random.randint(key, shape, 0, 2 ** 20) * (2 * REACH) + lax.broadcasted_iota(jnp.int32, shape, 2)
    ranked = jnp.argsort(scores, axis=2, stable=True)[:, :, :wanted].astype(jnp.int32)
    offsets = jnp.where(ranked < REACH, ranked - REACH, ranked - REACH + 1)
    home = lax.broadcasted_iota(jnp.int32, (SUBTREES, LEAVES, wanted), 1)
    target = home + offsets
    inside = (target >= 0) & (target < LEAVES)
    return jnp.where(inside, target, home - offsets)


def draw_near_cols(key, part):
    key = jax.random.fold_in(key, 11)
    others = window_partners(key, NEAR - 1)
    home = lax.broadcasted_iota(jnp.int32, (SUBTREES, LEAVES, 1), 1)
    return jnp.concatenate([home, others], axis=2)


def draw_leaf_src(key, part):
    key = jax.random.fold_in(key, 12)
    return window_partners(key, COUP0)


def draw_near_count(key, part):
    key = jax.random.fold_in(key, 13)
    first_key, second_key = jax.random.split(key)
    counts = jax.random.randint(first_key, (SUBTREES, LEAVES), 1, NEAR + 1)
    chosen = jax.random.randint(second_key, (SUBTREES, 1), 0, LEAVES)
    leaf_ids = lax.broadcasted_iota(jnp.int32, (SUBTREES, LEAVES), 1)
    return jnp.where(leaf_ids == chosen, NEAR, counts).astype(jnp.int32)


def draw_par_src(key, part):
    key = jax.random.fold_in(key, 14)
    first_key, second_key, third_key = jax.random.split(key, 3)
    cluster_count = PARENTS // PAR_DEV
    entries = PAR_DEV * COUP1
    shape = (SUBTREES, cluster_count, TOPS)
    scores = jax.random.randint(first_key, shape, 0, 2 ** 20) * TOPS + lax.broadcasted_iota(jnp.int32, shape, 2)
    device_order = jnp.argsort(scores, axis=2, stable=True).astype(jnp.int32)
    entry_ids = jnp.arange(entries, dtype=jnp.int32)
    which = jnp.where(entry_ids == entries - 1, 0, entry_ids % TOPS)
    targets = jnp.take(device_order, which, axis=2)
    shape_two = (SUBTREES, cluster_count, entries)
    shuffle = jax.random.randint(second_key, shape_two, 0, 2 ** 20) * entries + lax.broadcasted_iota(jnp.int32, shape_two, 2)
    shuffle = jnp.argsort(shuffle, axis=2, stable=True).astype(jnp.int32)
    targets = jnp.take_along_axis(targets, shuffle, axis=2)
    within = jax.random.randint(third_key, shape_two, 0, PAR_DEV)
    source_tree = targets // cluster_count
    source_clus = targets % cluster_count
    global_parent = source_tree * PARENTS + source_clus * PAR_DEV + within
    return global_parent.reshape(SUBTREES, PARENTS, COUP1).astype(jnp.int32)


def place_ends(result, key, smallest, high):
    spot = [jax.random.randint(jax.random.fold_in(key, axis), (), 0, length) for axis, length in enumerate(result.shape)]
    main_axis = result.shape.index(max(result.shape))
    next_to = spot[:main_axis] + [(spot[main_axis] + 1) % result.shape[main_axis]] + spot[main_axis + 1:]
    return result.at[tuple(spot)].set(smallest).at[tuple(next_to)].set(high)


def steps_of(stream_key, shape, cuts, least, top_value):
    gain, own = 1.0, jax.random.fold_in(stream_key, 6)
    for dim, shards_of in cuts:
        heights = jnp.exp(jax.random.uniform(jax.random.fold_in(own, dim), (shards_of,), jnp.float32, least / len(cuts), top_value / len(cuts)))
        gain = gain * jnp.repeat(heights, shape[dim] // shards_of).reshape([-1 if axis == dim else 1 for axis in range(len(shape))])
    return gain


def noise(own_key, shape, spread, reach, cuts=(), held_as=jnp.bfloat16):
    result = spread * jax.random.normal(own_key, shape, jnp.float32)
    if cuts:
        result = result * steps_of(own_key, shape, cuts, -0.22, 0.18)
    return jnp.clip(result, -reach, reach).astype(held_as)


def setup_inputs(seed: int = 0) -> dict:
    streams_of = jax.random.split(jax.random.key(seed), 14)
    right_sides = noise(streams_of[0], (R, SUBTREES, PTS), 1.0, 6.0, ((1, 8), (2, 16)))
    near_blocks = noise(streams_of[1], (SUBTREES, LEAVES, NEAR, B, B), (NEAR * B) ** -0.5, 0.15625, ((0, 8), (1, 16)))
    near_cols = draw_near_cols(jax.random.fold_in(streams_of[13], 71), 0)
    near_count = draw_near_count(jax.random.fold_in(streams_of[13], 71), 0)
    basis = noise(streams_of[4], (SUBTREES, LEAVES, B, K), B ** -0.5, 0.375, ((0, 8), (1, 16)))
    leaf_transfer = noise(streams_of[5], (SUBTREES, LEAVES, K, K), K ** -0.5, 0.75, ((0, 8), (1, 16)))
    par_transfer = noise(streams_of[6], (SUBTREES, PARENTS, K, K), K ** -0.5, 0.75, ((0, 8), (1, 16)))
    leaf_src = draw_leaf_src(jax.random.fold_in(streams_of[13], 71), 0)
    leaf_coup = noise(streams_of[8], (SUBTREES, LEAVES, COUP0, K, K), (COUP0 * K) ** -0.5, 0.25, ((0, 8), (1, 16)))
    par_src = draw_par_src(jax.random.fold_in(streams_of[13], 71), 0)
    par_coup = noise(streams_of[10], (SUBTREES, PARENTS, COUP1, K, K), (COUP1 * K) ** -0.5, 0.15625, ((0, 8), (1, 16)))
    top_src = place_ends(jax.random.randint(streams_of[11], (SUBTREES, N_CLUS, COUP2), 0, TOPS), jax.random.fold_in(streams_of[11], 1), 0, TOPS - 1).astype(jnp.int32)
    top_coup = noise(streams_of[12], (SUBTREES, N_CLUS, COUP2, K, K), (COUP2 * K) ** -0.5, 0.15625, ((0, 8), (1, 16)))
    return dict(right_sides=right_sides, near_blocks=near_blocks, near_cols=near_cols, near_count=near_count, basis=basis, leaf_transfer=leaf_transfer, par_transfer=par_transfer, leaf_src=leaf_src, leaf_coup=leaf_coup, par_src=par_src, par_coup=par_coup, top_src=top_src, top_coup=top_coup)


def near_subtree(packed):
    values, blocks, columns, counts = packed
    picked = values[:, columns, :].astype(jnp.float32)
    slot_ids = jnp.arange(NEAR)
    live_mask = (slot_ids[None, :] < counts[:, None]).astype(jnp.float32)
    picked = picked * live_mask[None, :, :, None]
    return jnp.einsum('rlnb,lnbc->rlc', picked, blocks.astype(jnp.float32))


def select_rows(table, positions):
    return table[positions]


def reference(right_sides, near_blocks, near_cols, near_count, basis, leaf_transfer, par_transfer, leaf_src, leaf_coup, par_src, par_coup, top_src, top_coup):
    leaves = right_sides.reshape(R, SUBTREES, LEAVES, B)
    leaf_coeff = jnp.einsum('rslb,slbk->slrk', leaves.astype(jnp.float32), basis.astype(jnp.float32)).astype(jnp.bfloat16)
    parent_coeff = jnp.einsum('spcrk,spckm->sprm', leaf_coeff.reshape(SUBTREES, PARENTS, 4, R, K).astype(jnp.float32), leaf_transfer.reshape(SUBTREES, PARENTS, 4, K, K).astype(jnp.float32)).astype(jnp.bfloat16)
    top_coeff = jnp.einsum('scprk,scpkm->scrm', parent_coeff.reshape(SUBTREES, N_CLUS, PAR_DEV, R, K).astype(jnp.float32), par_transfer.reshape(SUBTREES, N_CLUS, PAR_DEV, K, K).astype(jnp.float32)).astype(jnp.bfloat16)
    top_sources = top_coeff.reshape(TOPS, R, K)[top_src]
    top_field = jnp.einsum('scjrk,scjkm->scrm', top_sources.astype(jnp.float32), top_coup.astype(jnp.float32)).astype(jnp.bfloat16)
    par_sources = parent_coeff.reshape(SUBTREES * PARENTS, R, K)[par_src]
    par_field = jnp.einsum('spjrk,spjkm->sprm', par_sources.astype(jnp.float32), par_coup.astype(jnp.float32))
    top_down = jnp.repeat(top_field, PAR_DEV, axis=1).astype(jnp.float32)
    par_field = (par_field + jnp.einsum('sprm,spkm->sprk', top_down, par_transfer.astype(jnp.float32))).astype(jnp.bfloat16)
    leaf_sources = jax.vmap(select_rows)(leaf_coeff, leaf_src)
    leaf_field = jnp.einsum('sljrk,sljkm->slrm', leaf_sources.astype(jnp.float32), leaf_coup.astype(jnp.float32))
    par_down = jnp.repeat(par_field, 4, axis=1).astype(jnp.float32)
    leaf_field = (leaf_field + jnp.einsum('slrm,slkm->slrk', par_down, leaf_transfer.astype(jnp.float32))).astype(jnp.bfloat16)
    far_sum = jnp.einsum('slrk,slbk->rslb', leaf_field.astype(jnp.float32), basis.astype(jnp.float32))
    near_sum = lax.map(near_subtree, (jnp.moveaxis(leaves, 1, 0), near_blocks, near_cols, near_count))
    near_sum = jnp.moveaxis(near_sum, 0, 1)
    return (near_sum + far_sum).reshape(R, SUBTREES, PTS).astype(jnp.bfloat16)
```

```python
import jax
import jax.numpy as jnp
from jax import lax
from jax.experimental import pallas as pl
from jax.experimental.pallas import tpu as pltpu
from jax.sharding import PartitionSpec as P

F32 = jnp.float32
BF16 = jnp.bfloat16
LEAVES = 24
PARENTS = 6
HALO = 8
NEAR = 5
PTS = 256
ZERO = LEAVES + 2 * HALO
PARTS = (((0, 2), "xyz"), ((2, 2), "yzx"), ((4, 2), "zxy"), (None, "xyz"))


def dot(a, b):
    return lax.dot_general(a, b, (((1,), (0,)), ((), ())), preferred_element_type=F32)


def dot_t(a, b):
    return lax.dot_general(a, b, (((1,), (1,)), ((), ())), preferred_element_type=F32)


def pack(y):
    return jnp.concatenate([y[:16], y[16:]], axis=1).astype(BF16)


def side_by_side(tiles):
    low = lax.broadcasted_iota(jnp.int32, (16, 128), 1) < 64
    columns = []
    for i in range(0, len(tiles), 2):
        a = tiles[i].astype(F32)
        b = tiles[i + 1].astype(F32) if i + 1 < len(tiles) else jnp.zeros_like(a)
        top = jnp.where(low, a, pltpu.roll(b, 64, 1))
        bottom = jnp.where(low, pltpu.roll(a, 64, 1), b)
        columns.append(jnp.concatenate([top, bottom], axis=0).astype(BF16))
    return jnp.concatenate(columns, axis=1)


def kernel(
    rhs, near, cols, count, basis, lt, pt, leaf_src, leaf_coup, par_src, par_coup, top_src, top_coup,
    out,
    x_v, near_v, basis_v, lt_v, pt_v, leaf_coup_v, par_coup_v, top_coup_v, out_v,
    cols_s, count_s, leaf_src_s, par_src_s, top_src_s,
    leaf_t, par_t, top_t, near_acc, leaf_acc,
    x_sem, in_sem, near_sem, halo_send, halo_recv, ag_send, ag_recv, core_send, core_recv, out_sem,
):
    clus = lax.axis_index("clus")
    tree = lax.axis_index("leaf")
    y, x = lax.div(clus, 4), lax.rem(clus, 4)
    z, core = lax.div(tree, 2), lax.rem(tree, 2)

    def device(dz=0, dc=0, dy=0, dx=0):
        return (
            lax.rem(y + dy, 4) * 4 + lax.rem(x + dx, 4),
            lax.rem(z + dz, 4) * 2 + lax.rem(core + dc, 2),
        )

    right, left = (lax.rem(clus + 1, 16), tree), (lax.rem(clus + 15, 16), tree)
    sibling = device(dc=1)
    along = {
        "z": [device(dz=d) for d in (1, 2, 3)],
        "y": [device(dy=d) for d in (1, 2, 3)],
        "x": [device(dx=d) for d in (1, 2, 3)],
    }
    partners = [right, left, sibling] + along["z"] + along["y"] + along["x"]
    barrier = pltpu.get_barrier_semaphore()
    for partner in partners:
        pl.semaphore_signal(barrier, inc=1, device_id=partner, device_id_type=pl.DeviceIdType.MESH)

    def fetch(i, src, dst):
        return pltpu.make_async_copy(src, dst, in_sem.at[i])

    def x_fetch(g):
        return pltpu.make_async_copy(rhs.at[:, pl.ds(g * PTS, PTS)], x_v.at[HALO + g], x_sem.at[g])

    for g in range(LEAVES):
        x_fetch(g).start()
    fetches = [
        fetch(1, basis, basis_v),
        fetch(2, lt, lt_v),
        fetch(3, pt, pt_v),
        fetch(4, cols, cols_s),
        fetch(5, count, count_s),
        fetch(6, leaf_src, leaf_src_s),
        fetch(7, par_src, par_src_s),
        fetch(8, top_src, top_src_s),
        fetch(9, leaf_coup, leaf_coup_v),
        fetch(10, par_coup, par_coup_v),
        fetch(11, top_coup, top_coup_v),
    ]
    for f in fetches[:3]:
        f.start()

    def near_fetch(g):
        return pltpu.make_async_copy(near.at[g], near_v.at[g], near_sem.at[g])

    @pl.loop(0, LEAVES)
    def _(g):
        near_fetch(g).start()

    for f in fetches[3:]:
        f.start()

    def remote(src, dst, send, recv, to):
        return pltpu.make_async_remote_copy(
            src_ref=src, dst_ref=dst, send_sem=send, recv_sem=recv, device_id=to,
            device_id_type=pl.DeviceIdType.MESH,
        )

    x_v[ZERO] = jnp.zeros((32, PTS), BF16)
    pl.semaphore_wait(barrier, len(partners))
    halos = [
        remote(x_v.at[pl.ds(LEAVES, HALO)], x_v.at[pl.ds(0, HALO)], halo_send.at[0], halo_recv.at[0], right),
        remote(x_v.at[pl.ds(HALO, HALO)], x_v.at[pl.ds(LEAVES + HALO, HALO)], halo_send.at[1], halo_recv.at[1], left),
        remote(leaf_t.at[pl.ds(LEAVES, HALO)], leaf_t.at[pl.ds(0, HALO)], halo_send.at[2], halo_recv.at[2], right),
        remote(leaf_t.at[pl.ds(HALO, HALO)], leaf_t.at[pl.ds(LEAVES + HALO, HALO)], halo_send.at[3], halo_recv.at[3], left),
    ]
    for g in range(LEAVES):
        x_fetch(g).wait()
    halos[0].start()
    halos[1].start()
    for f in fetches[:2]:
        f.wait()

    for g in range(LEAVES):
        leaf_t[HALO + g] = pack(dot_t(x_v[HALO + g], basis_v[g]))
    halos[2].start()
    halos[3].start()
    own = par_t.at[z, core, y, x]
    parent_tiles = []
    for p in range(PARENTS):
        lhs = side_by_side([leaf_t[HALO + 4 * p + c] for c in range(4)])
        tile = pack(dot(lhs, lt_v[4 * p:4 * p + 4].reshape(256, 64)))
        parent_tiles.append(tile)
        own[p] = tile
    fetches[2].wait()
    lhs = side_by_side(parent_tiles)
    top_t[z, core, y, x] = pack(dot(lhs, pt_v[...].reshape(PARENTS * 64, 64)))

    def block(part, done):
        rows = PARTS[part][0]
        at = tuple(
            slice(None) if name in done else value
            for name, value in (("z", z), ("core", core), ("y", y), ("x", x))
        )
        if rows is None:
            return top_t.at[at]
        return par_t.at[at + (pl.ds(rows[0], rows[1]),)]

    def hop(part, stage, k):
        order = PARTS[part][1]
        ref = block(part, order[:stage])
        i = (part * 3 + stage) * 3 + k
        return remote(ref, ref, ag_send.at[i], ag_recv.at[i], along[order[stage]][k])

    def stage_start(stage):
        for part in (3, 0, 1, 2):
            for k in range(3):
                hop(part, stage, k).start()

    def stage_wait(stage):
        for part in (3, 0, 1, 2):
            for k in range(3):
                hop(part, stage, k).wait_recv()

    stage_start(0)

    first = clus * LEAVES - HALO

    def near_leaf(g):
        near_fetch(g).wait()
        total = None
        for n in range(NEAR):
            live = jnp.clip(count_s[0, g] - n, 0, 1)
            at = ZERO + live * (jnp.clip(cols_s[n, 0, g] - first, 0, ZERO - 1) - ZERO)
            term = dot(x_v[at], near_v[g, n])
            total = term if total is None else total + term
        near_acc[g] = total

    for f in fetches[3:8]:
        f.wait()
    halos[0].wait()
    halos[1].wait()

    def near_range(lo, hi):
        @pl.loop(lo, hi)
        def _(g):
            near_leaf(g)

    near_range(0, 4)
    stage_wait(0)
    stage_start(1)
    near_range(4, 9)
    stage_wait(1)
    stage_start(2)

    def plane_relay(part):
        ref = block(part, PARTS[part][1][:2])
        return remote(ref, ref, core_send.at[part * 4], core_recv.at[part * 4], sibling)

    def last_relay(part, k):
        axis = PARTS[part][1][2]
        here = {"z": z, "y": y, "x": x}
        here[axis] = lax.rem(here[axis] + 3 - k, 4)
        done = PARTS[part][1][:2]
        at = tuple(
            slice(None) if name in done else value
            for name, value in (("z", here["z"]), ("core", core), ("y", here["y"]), ("x", here["x"]))
        )
        rows = PARTS[part][0]
        ref = top_t.at[at] if rows is None else par_t.at[at + (pl.ds(rows[0], rows[1]),)]
        i = part * 4 + 1 + k
        return remote(ref, ref, core_send.at[i], core_recv.at[i], sibling)

    for part in (3, 0, 1, 2):
        plane_relay(part).start()

    near_range(9, 24)

    halos[2].wait()
    halos[3].wait()
    fetches[8].wait()

    @pl.loop(0, PARENTS)
    def _(p):
        fields = []
        for c in range(4):
            g = 4 * p + c
            total = None
            for half in range(2):
                tiles = []
                for j in range(4 * half, 4 * half + 4):
                    tiles.append(leaf_t[jnp.clip(leaf_src_s[j, g] - first, 0, ZERO - 1)])
                term = dot(side_by_side(tiles), leaf_coup_v[g, 4 * half:4 * half + 4].reshape(256, 64))
                total = term if total is None else total + term
            fields.append(total)
        leaf_acc[p] = jnp.concatenate(fields, axis=1)

    for k in (0, 2, 1):
        for part in (3, 0, 1, 2):
            hop(part, 2, k).wait_recv()
            last_relay(part, k).start()
    for part in (3, 0, 1, 2):
        plane_relay(part).wait_recv()
        for k in (0, 2, 1):
            last_relay(part, k).wait_recv()

    fetches[10].wait()
    total = None
    for j in range(0, 27, 4):
        tiles = []
        for i in range(j, min(j + 4, 27)):
            t = top_src_s[0, 0, i]
            tiles.append(top_t[t >> 5, (t >> 4) & 1, (t >> 2) & 3, t & 3])
        weights = top_coup_v[j:j + len(tiles)].reshape(len(tiles) * 64, 64)
        term = dot(side_by_side(tiles)[:, :len(tiles) * 64], weights)
        total = term if total is None else total + term
    top_field = total.astype(BF16)
    top_down = dot_t(top_field, pt_v[...].reshape(PARENTS * 64, 64))
    fetches[9].wait()
    lane = lax.broadcasted_iota(jnp.int32, (32, 256), 1) // 64
    for p in range(PARENTS):
        total = top_down[:, 64 * p:64 * p + 64]
        for j in range(0, 27, 4):
            tiles = []
            for i in range(j, min(j + 4, 27)):
                q = par_src_s[p, 0, i]
                d = lax.div(q, PARENTS)
                tiles.append(par_t[d >> 5, (d >> 4) & 1, (d >> 2) & 3, d & 3, q - d * PARENTS])
            weights = par_coup_v[p, j:j + len(tiles)].reshape(len(tiles) * 64, 64)
            total = total + dot(side_by_side(tiles)[:, :len(tiles) * 64], weights)
        field = leaf_acc[p] + dot_t(total.astype(BF16), lt_v[4 * p:4 * p + 4].reshape(256, 64))
        field = field.astype(BF16)
        spread = jnp.concatenate(
            [jnp.where(lane == c, field, jnp.zeros_like(field)) for c in range(4)], axis=0
        )
        far = dot(spread, basis_v[4 * p:4 * p + 4].reshape(256, 256))
        for c in range(4):
            g = 4 * p + c
            out_v[:, g * PTS:(g + 1) * PTS] = (near_acc[g] + far[32 * c:32 * c + 32]).astype(BF16)
    write = pltpu.make_async_copy(out_v, out, out_sem)
    write.start()

    for part in range(4):
        for stage in range(3):
            for k in range(3):
                hop(part, stage, k).wait_send()
        plane_relay(part).wait_send()
        for k in range(3):
            last_relay(part, k).wait_send()
    write.wait()


def local(
    right_sides, near_blocks, near_cols, near_count, basis, leaf_transfer, par_transfer,
    leaf_src, leaf_coup, par_src, par_coup, top_src, top_coup,
):
    vma = pltpu.VMEM
    call = pl.pallas_call(
        kernel,
        out_shape=jax.ShapeDtypeStruct((32, LEAVES * PTS), BF16),
        in_specs=[pl.BlockSpec(memory_space=pl.ANY)] * 13,
        out_specs=pl.BlockSpec(memory_space=pl.ANY),
        scratch_shapes=[
            vma((ZERO + 1, 32, PTS), BF16),
            vma((LEAVES, NEAR, PTS, PTS), BF16),
            vma((LEAVES, 64, PTS), BF16),
            vma((LEAVES, 64, 64), BF16),
            vma((PARENTS, 64, 64), BF16),
            vma((LEAVES, 8, 64, 64), BF16),
            vma((PARENTS, 27, 64, 64), BF16),
            vma((27, 64, 64), BF16),
            vma((32, LEAVES * PTS), BF16),
            pltpu.SMEM((NEAR, 1, LEAVES), jnp.int32),
            pltpu.SMEM((1, LEAVES), jnp.int32),
            pltpu.SMEM((8, LEAVES), jnp.int32),
            pltpu.SMEM((PARENTS, 1, 27), jnp.int32),
            pltpu.SMEM((1, 1, 27), jnp.int32),
            vma((LEAVES + 2 * HALO, 16, 128), BF16),
            vma((4, 2, 4, 4, PARENTS, 16, 128), BF16),
            vma((4, 2, 4, 4, 16, 128), BF16),
            vma((LEAVES, 32, PTS), F32),
            vma((PARENTS, 32, PTS), F32),
            pltpu.SemaphoreType.DMA((LEAVES,)),
            pltpu.SemaphoreType.DMA((12,)),
            pltpu.SemaphoreType.DMA((LEAVES,)),
            pltpu.SemaphoreType.DMA((4,)),
            pltpu.SemaphoreType.DMA((4,)),
            pltpu.SemaphoreType.DMA((36,)),
            pltpu.SemaphoreType.DMA((36,)),
            pltpu.SemaphoreType.DMA((16,)),
            pltpu.SemaphoreType.DMA((16,)),
            pltpu.SemaphoreType.DMA,
        ],
        compiler_params=pltpu.CompilerParams(
            collective_id=0, has_side_effects=True, vmem_limit_bytes=63 * 2**20
        ),
    )
    out = call(
        right_sides[:, 0],
        near_blocks[0],
        jnp.transpose(near_cols, (2, 0, 1)),
        near_count,
        jnp.swapaxes(basis[0], 1, 2),
        leaf_transfer[0],
        par_transfer[0],
        jnp.transpose(leaf_src[0], (1, 0)),
        leaf_coup[0],
        jnp.transpose(par_src, (1, 0, 2)),
        par_coup[0],
        top_src,
        top_coup[0, 0],
    )
    return out[:, None, :]


def solution(mesh):
    return jax.shard_map(
        local,
        mesh=mesh,
        in_specs=(
            P(None, "leaf", "clus"),
            P("leaf", "clus", None, None, None),
            P("leaf", "clus", None),
            P("leaf", "clus"),
            P("leaf", "clus", None, None),
            P("leaf", "clus", None, None),
            P("leaf", "clus", None, None),
            P("leaf", "clus", None),
            P("leaf", "clus", None, None, None),
            P("leaf", "clus", None),
            P("leaf", "clus", None, None, None),
            P("leaf", "clus", None),
            P("leaf", "clus", None, None, None),
        ),
        out_specs=P(None, "leaf", "clus"),
        check_vma=False,
    )
```

```python
import jax
import jax.numpy as jnp
from jax import lax
from jax.experimental import pallas as pl
from jax.experimental.pallas import tpu as pltpu
from jax.sharding import PartitionSpec as P

F32 = jnp.float32
BF16 = jnp.bfloat16
LEAVES = 24
PARENTS = 6
HALO = 8
NEAR = 5
PTS = 256
ZERO = LEAVES + 2 * HALO
ORDERS = ("xyz", "yzx", "zxy")
ALL = (3, 0, 1, 2)
TOP = 3


def dot(a, b):
    return lax.dot_general(a, b, (((1,), (0,)), ((), ())), preferred_element_type=F32)


def dot_t(a, b):
    return lax.dot_general(a, b, (((1,), (1,)), ((), ())), preferred_element_type=F32)


def pack(y):
    return jnp.concatenate([y[:16], y[16:]], axis=1).astype(BF16)


def side_by_side(tiles):
    low = lax.broadcasted_iota(jnp.int32, (16, 128), 1) < 64
    columns = []
    for i in range(0, len(tiles), 2):
        a = tiles[i].astype(F32)
        b = tiles[i + 1].astype(F32) if i + 1 < len(tiles) else jnp.zeros_like(a)
        top = jnp.where(low, a, pltpu.roll(b, 64, 1))
        bottom = jnp.where(low, pltpu.roll(a, 64, 1), b)
        columns.append(jnp.concatenate([top, bottom], axis=0).astype(BF16))
    return jnp.concatenate(columns, axis=1)


def kernel(
    rhs, near, cols, count, basis, lt, pt, leaf_src, leaf_coup, par_src, par_coup, top_src, top_coup,
    out,
    x_own, x_v, near_v, basis_v, lt_v, pt_v, leaf_coup_v, par_coup_v, top_coup_v, out_v,
    cols_s, count_s, leaf_src_s, par_src_s, top_src_s,
    leaf_t, par_t, top_t, near_acc, leaf_acc,
    x_sem, in_sem, near_sem, halo_send, halo_recv, own_sem,
    spread_send, spread_recv, across_send, across_recv, onward_send, onward_recv,
    forward_send, forward_recv, share_send, share_recv, out_sem,
):
    clus = lax.axis_index("clus")
    tree = lax.axis_index("leaf")
    y, x = lax.div(clus, 4), lax.rem(clus, 4)
    z, core = lax.div(tree, 2), lax.rem(tree, 2)

    def device(dz=0, dc=0, dy=0, dx=0):
        return (
            lax.rem(y + dy, 4) * 4 + lax.rem(x + dx, 4),
            lax.rem(z + dz, 4) * 2 + lax.rem(core + dc, 2),
        )

    ta, tb, tc = x + core * (y - x), y + core * (z - y), z + core * (x - z)

    right, left = (lax.rem(clus + 1, 16), tree), (lax.rem(clus + 15, 16), tree)
    sibling = device(dc=1)
    along = {
        "z": [device(dz=d) for d in (1, 2, 3)],
        "y": [device(dy=d) for d in (1, 2, 3)],
        "x": [device(dx=d) for d in (1, 2, 3)],
    }
    partners = [right, left, sibling] + along["z"] + along["y"] + along["x"]
    barrier = pltpu.get_barrier_semaphore()
    for partner in partners:
        pl.semaphore_signal(barrier, inc=1, device_id=partner, device_id_type=pl.DeviceIdType.MESH)

    def fetch(i, src, dst):
        return pltpu.make_async_copy(src, dst, in_sem.at[i])

    def x_fetch(g):
        return pltpu.make_async_copy(rhs.at[:, pl.ds(g * PTS, PTS)], x_own.at[g], x_sem)

    for g in range(LEAVES):
        x_fetch(g).start()
    fetches = [
        fetch(1, basis, basis_v),
        fetch(2, lt, lt_v),
        fetch(3, pt, pt_v),
        fetch(4, cols, cols_s),
        fetch(5, count, count_s),
        fetch(6, leaf_src, leaf_src_s),
        fetch(7, par_src, par_src_s),
        fetch(8, top_src, top_src_s),
        fetch(9, leaf_coup, leaf_coup_v),
        fetch(10, par_coup, par_coup_v),
        fetch(11, top_coup, top_coup_v),
    ]
    for f in fetches[:3]:
        f.start()

    def near_fetch(i):
        pair = pl.ds(2 * i, 2)
        return pltpu.make_async_copy(near.at[pair], near_v.at[pair], near_sem.at[i])

    @pl.loop(0, LEAVES // 2)
    def _(i):
        near_fetch(i).start()

    for f in fetches[3:]:
        f.start()

    def remote(src, dst, send, recv, to):
        return pltpu.make_async_remote_copy(
            src_ref=src, dst_ref=dst, send_sem=send, recv_sem=recv, device_id=to,
            device_id_type=pl.DeviceIdType.MESH,
        )

    x_v[ZERO] = jnp.zeros((32, PTS), BF16)
    x_own[LEAVES] = jnp.zeros((32, PTS), BF16)
    pl.semaphore_wait(barrier, len(partners))
    def halo(i, own, table):
        lo, hi = pl.ds(0, HALO), pl.ds(LEAVES + HALO, HALO)
        return [
            remote(own.at[pl.ds(own.shape[0] - HALO, HALO)], table.at[lo], halo_send.at[i], halo_recv.at[i], right),
            remote(own.at[lo], table.at[hi], halo_send.at[i], halo_recv.at[i], left),
        ]

    def halo_wait(i, table):
        both = table.at[pl.ds(0, 2 * HALO)]
        remote(both, both, halo_send.at[i], halo_recv.at[i], right).wait()

    x_halos = halo(0, x_own.at[pl.ds(0, LEAVES)], x_v)
    leaf_halos = halo(1, leaf_t.at[pl.ds(HALO, LEAVES)], leaf_t)
    own = x_own.at[pl.ds(0, LEAVES)]
    pltpu.make_async_copy(own, own, x_sem).wait()
    for c in x_halos:
        c.start()
    own_copy = pltpu.make_async_copy(x_own.at[pl.ds(0, LEAVES)], x_v.at[pl.ds(HALO, LEAVES)], own_sem)
    own_copy.start()
    for f in fetches[:2]:
        f.wait()

    def unit(part):
        if part == TOP:
            return top_t.at[core, tc, tb, ta]
        return par_t.at[z, core, y, x, pl.ds(2 * part, 2)]

    def row(part, r, d):
        if part == TOP:
            return top_t.at[core, lax.rem(tc + 4 - d, 4), lax.rem(tb + 4 - r, 4)]
        a, b, c = ORDERS[part]
        at = {"z": z, "y": y, "x": x}
        at[b], at[c] = lax.rem(at[b] + 4 - r, 4), lax.rem(at[c] + 4 - d, 4)
        at[a] = slice(None)
        return par_t.at[at["z"], core, at["y"], at["x"], pl.ds(2 * part, 2)]

    def target(part, axis, d):
        if part == TOP:
            one, two = ("xyz"[axis], "yzx"[axis])
            return device(**{"d" + one: d * (1 - core), "d" + two: d * core})
        return along[ORDERS[part][axis]][d - 1]

    def kind(part):
        return int(part == TOP)

    def spread(part, k):
        i = kind(part)
        return remote(unit(part), unit(part), spread_send.at[i], spread_recv.at[i], target(part, 0, k + 1))

    def across(part, k):
        i = kind(part)
        ref = row(part, 0, 0)
        return remote(ref, ref, across_send.at[i], across_recv.at[i * 3 + k], target(part, 1, k + 1))

    def onward(part, r, way):
        i = kind(part)
        ref = row(part, r, 0)
        return remote(ref, ref, onward_send.at[i], onward_recv.at[i * 4 + r], target(part, 2, (1, 3)[way]))

    def forward(part, r):
        i = kind(part)
        d = 1 if r in (0, 3) else 3
        ref = row(part, r, d)
        return remote(ref, ref, forward_send.at[i], forward_recv.at[i * 4 + r], target(part, 2, d))

    def share(part, r, d):
        i = kind(part)
        ref = row(part, r, d)
        return remote(ref, ref, share_send.at[i], share_recv.at[i], sibling)

    def received(semaphore, ref):
        pltpu.make_async_copy(ref, ref, semaphore).wait()

    def rows(i, n):
        if i == 1:
            return top_t.at[core, 0, pl.ds(0, n)]
        return par_t.at[0, core, pl.ds(0, n)]

    for g in range(LEAVES):
        leaf_t[HALO + g] = pack(dot_t(x_own[g], basis_v[g]))
    for c in leaf_halos:
        c.start()
    parent_tiles = []
    for p in range(PARENTS):
        lhs = side_by_side([leaf_t[HALO + 4 * p + c] for c in range(4)])
        tile = pack(dot(lhs, lt_v[4 * p:4 * p + 4].reshape(256, 64)))
        parent_tiles.append(tile)
        par_t[z, core, y, x, p] = tile
        if p % 2:
            for k in (1, 0, 2):
                spread(p // 2, k).start()

    fetches[2].wait()
    lhs = side_by_side(parent_tiles)
    top_t[core, tc, tb, ta] = pack(dot(lhs, pt_v[...].reshape(PARENTS * 64, 64)))
    for k in (1, 0, 2):
        spread(TOP, k).start()

    first = clus * LEAVES - HALO

    def near_leaf(g, table, first, end):
        total = None
        for n in range(NEAR):
            live = jnp.clip(count_s[0, g] - n, 0, 1)
            at = end + live * (jnp.clip(cols_s[n, 0, g] - first, 0, end - 1) - end)
            term = dot(table[at], near_v[g, n])
            total = term if total is None else total + term
        near_acc[g] = total

    for f in fetches[3:8]:
        f.wait()

    def near_inner(lo, hi):
        @pl.loop(lo, hi)
        def _(i):
            near_fetch(i).wait()
            for g in (2 * i, 2 * i + 1):
                near_leaf(g, x_own, clus * LEAVES, LEAVES)

    def near_outer(lo, hi):
        @pl.loop(lo, hi)
        def _(i):
            near_fetch(i).wait()
            for g in (2 * i, 2 * i + 1):
                near_leaf(g, x_v, first, ZERO)

    near_inner(4, 6)
    received(spread_recv.at[0], par_t.at[0, core, 0, pl.ds(0, 3)])
    received(spread_recv.at[1], top_t.at[core, 0, 0, pl.ds(0, 3)])
    for part in ALL:
        for k in (0, 2, 1):
            across(part, k).start()
        for way in (0, 1):
            onward(part, 0, way).start()
        share(part, 0, 0).start()
    near_inner(6, 8)
    for r in (1, 3, 2):
        for i in (1, 0):
            received(across_recv.at[i * 3 + r - 1], rows(i, 1))
        for part in ALL:
            for way in (0, 1):
                onward(part, r, way).start()
            share(part, r, 0).start()
    own_copy.wait()
    halo_wait(0, x_v)
    for step, r in enumerate((0, 1, 3, 2)):
        lo = (8, 10, 0, 2)[step]
        near_outer(lo, lo + 2)
        for i in (1, 0):
            received(onward_recv.at[i * 4 + r], rows(i, 2))
        for part in ALL:
            forward(part, r).start()
            share(part, r, 1).start()
            share(part, r, 3).start()

    halo_wait(1, leaf_t)
    fetches[8].wait()

    @pl.loop(0, PARENTS)
    def _(p):
        fields = []
        for c in range(4):
            g = 4 * p + c
            total = None
            for half in range(2):
                tiles = []
                for j in range(4 * half, 4 * half + 4):
                    tiles.append(leaf_t[jnp.clip(leaf_src_s[j, g] - first, 0, ZERO - 1)])
                term = dot(side_by_side(tiles), leaf_coup_v[g, 4 * half:4 * half + 4].reshape(256, 64))
                total = term if total is None else total + term
            fields.append(total)
        leaf_acc[p] = jnp.concatenate(fields, axis=1)

    for r in (0, 1, 3, 2):
        for i in (1, 0):
            received(forward_recv.at[i * 4 + r], rows(i, 1))
        for part in ALL:
            share(part, r, 2).start()
    received(share_recv.at[1], top_t.at[0])
    received(share_recv.at[0], par_t.at[:, 0])

    fetches[10].wait()
    total = None
    for j in range(0, 27, 4):
        tiles = []
        for i in range(j, min(j + 4, 27)):
            t = top_src_s[0, 0, i]
            tz, tcore, ty, tx = t >> 5, (t >> 4) & 1, (t >> 2) & 3, t & 3
            tiles.append(top_t[tcore, tz + tcore * (tx - tz), ty + tcore * (tz - ty), tx + tcore * (ty - tx)])
        weights = top_coup_v[j:j + len(tiles)].reshape(len(tiles) * 64, 64)
        term = dot(side_by_side(tiles)[:, :len(tiles) * 64], weights)
        total = term if total is None else total + term
    top_field = total.astype(BF16)
    all_parents = par_t.reshape(768, 16, 128)
    top_down = dot_t(top_field, pt_v[...].reshape(PARENTS * 64, 64))
    fetches[9].wait()
    lane = lax.broadcasted_iota(jnp.int32, (32, 256), 1) // 64
    for p in range(PARENTS):
        total = top_down[:, 64 * p:64 * p + 64]
        for j in range(0, 27, 4):
            tiles = []
            for i in range(j, min(j + 4, 27)):
                q = par_src_s[p, 0, i]
                tiles.append(all_parents[q])
            weights = par_coup_v[p, j:j + len(tiles)].reshape(len(tiles) * 64, 64)
            total = total + dot(side_by_side(tiles)[:, :len(tiles) * 64], weights)
        field = leaf_acc[p] + dot_t(total.astype(BF16), lt_v[4 * p:4 * p + 4].reshape(256, 64))
        field = field.astype(BF16)
        masked = jnp.concatenate(
            [jnp.where(lane == c, field, jnp.zeros_like(field)) for c in range(4)], axis=0
        )
        far = dot(masked, basis_v[4 * p:4 * p + 4].reshape(256, 256))
        for c in range(4):
            g = 4 * p + c
            out_v[:, g * PTS:(g + 1) * PTS] = (near_acc[g] + far[32 * c:32 * c + 32]).astype(BF16)
        columns = pl.ds(4 * p * PTS, 4 * PTS)
        pltpu.make_async_copy(out_v.at[:, columns], out.at[:, columns], out_sem).start()

    for i, table in enumerate((par_t.at[:, core], top_t.at[core])):
        pieces = par_t.at[0, core, 0, pl.ds(0, 3)] if i == 0 else top_t.at[core, 0, 0, pl.ds(0, 3)]
        received(spread_send.at[i], pieces)
        received(across_send.at[i], rows(i, 3))
        received(onward_send.at[i], par_t.at[pl.ds(0, 2), core] if i == 0 else top_t.at[core, pl.ds(0, 2)])
        received(forward_send.at[i], rows(i, 4))
        received(share_send.at[i], table)
    received(out_sem, out_v)


def local(
    right_sides, near_blocks, near_cols, near_count, basis, leaf_transfer, par_transfer,
    leaf_src, leaf_coup, par_src, par_coup, top_src, top_coup,
):
    vma = pltpu.VMEM
    call = pl.pallas_call(
        kernel,
        out_shape=jax.ShapeDtypeStruct((32, LEAVES * PTS), BF16),
        in_specs=[pl.BlockSpec(memory_space=pl.ANY)] * 13,
        out_specs=pl.BlockSpec(memory_space=pl.ANY),
        scratch_shapes=[
            vma((LEAVES + 1, 32, PTS), BF16),
            vma((ZERO + 1, 32, PTS), BF16),
            vma((LEAVES, NEAR, PTS, PTS), BF16),
            vma((LEAVES, 64, PTS), BF16),
            vma((LEAVES, 64, 64), BF16),
            vma((PARENTS, 64, 64), BF16),
            vma((LEAVES, 8, 64, 64), BF16),
            vma((PARENTS, 27, 64, 64), BF16),
            vma((27, 64, 64), BF16),
            vma((32, LEAVES * PTS), BF16),
            pltpu.SMEM((NEAR, 1, LEAVES), jnp.int32),
            pltpu.SMEM((1, LEAVES), jnp.int32),
            pltpu.SMEM((8, LEAVES), jnp.int32),
            pltpu.SMEM((PARENTS, 1, 27), jnp.int32),
            pltpu.SMEM((1, 1, 27), jnp.int32),
            vma((LEAVES + 2 * HALO, 16, 128), BF16),
            vma((4, 2, 4, 4, PARENTS, 16, 128), BF16),
            vma((2, 4, 4, 4, 16, 128), BF16),
            vma((LEAVES, 32, PTS), F32),
            vma((PARENTS, 32, PTS), F32),
            pltpu.SemaphoreType.DMA,
            pltpu.SemaphoreType.DMA((12,)),
            pltpu.SemaphoreType.DMA((LEAVES // 2,)),
            pltpu.SemaphoreType.DMA((2,)),
            pltpu.SemaphoreType.DMA((2,)),
            pltpu.SemaphoreType.DMA,
            pltpu.SemaphoreType.DMA((2,)),
            pltpu.SemaphoreType.DMA((2,)),
            pltpu.SemaphoreType.DMA((2,)),
            pltpu.SemaphoreType.DMA((6,)),
            pltpu.SemaphoreType.DMA((2,)),
            pltpu.SemaphoreType.DMA((8,)),
            pltpu.SemaphoreType.DMA((2,)),
            pltpu.SemaphoreType.DMA((8,)),
            pltpu.SemaphoreType.DMA((2,)),
            pltpu.SemaphoreType.DMA((2,)),
            pltpu.SemaphoreType.DMA,
        ],
        compiler_params=pltpu.CompilerParams(
            collective_id=0, has_side_effects=True, vmem_limit_bytes=63 * 2**20
        ),
    )
    out = call(
        right_sides[:, 0],
        near_blocks[0],
        jnp.transpose(near_cols, (2, 0, 1)),
        near_count,
        jnp.swapaxes(basis[0], 1, 2),
        leaf_transfer[0],
        par_transfer[0],
        jnp.transpose(leaf_src[0], (1, 0)),
        leaf_coup[0],
        jnp.transpose(par_src, (1, 0, 2)),
        par_coup[0],
        top_src,
        top_coup[0, 0],
    )
    return out[:, None, :]


def solution(mesh):
    return jax.shard_map(
        local,
        mesh=mesh,
        in_specs=(
            P(None, "leaf", "clus"),
            P("leaf", "clus", None, None, None),
            P("leaf", "clus", None),
            P("leaf", "clus"),
            P("leaf", "clus", None, None),
            P("leaf", "clus", None, None),
            P("leaf", "clus", None, None),
            P("leaf", "clus", None),
            P("leaf", "clus", None, None, None),
            P("leaf", "clus", None),
            P("leaf", "clus", None, None, None),
            P("leaf", "clus", None),
            P("leaf", "clus", None, None, None),
        ),
        out_specs=P(None, "leaf", "clus"),
        check_vma=False,
    )
```

```python
import jax
import jax.numpy as jnp
from jax import lax
from jax.experimental import pallas as pl
from jax.experimental.pallas import tpu as pltpu
from jax.sharding import PartitionSpec as P

F32 = jnp.float32
BF16 = jnp.bfloat16
LEAVES = 24
PARENTS = 6
HALO = 8
NEAR = 5
PTS = 256
ZERO = LEAVES + 2 * HALO
ORDERS = ("xyz", "yzx", "zxy")
ALL = (3, 0, 1, 2)
QUADS = 7
TOP = 3


def dot(a, b):
    return lax.dot_general(a, b, (((1,), (0,)), ((), ())), preferred_element_type=F32)


def dot_t(a, b):
    return lax.dot_general(a, b, (((1,), (1,)), ((), ())), preferred_element_type=F32)


def pack(y):
    return jnp.concatenate([y[:16], y[16:]], axis=1).astype(BF16)


def side_by_side(tiles):
    low = lax.broadcasted_iota(jnp.int32, (16, 128), 1) < 64
    columns = []
    for i in range(0, len(tiles), 2):
        a = tiles[i].astype(F32)
        b = tiles[i + 1].astype(F32) if i + 1 < len(tiles) else jnp.zeros_like(a)
        top = jnp.where(low, a, pltpu.roll(b, 64, 1))
        bottom = jnp.where(low, pltpu.roll(a, 64, 1), b)
        columns.append(jnp.concatenate([top, bottom], axis=0).astype(BF16))
    return jnp.concatenate(columns, axis=1)


def kernel(
    rhs, near, cols, count, basis, lt, pt, leaf_src, leaf_coup, par_src, par_coup, top_src, top_coup,
    out,
    x_own, x_v, near_v, basis_v, lt_v, pt_v, leaf_coup_v, par_coup_v, top_coup_v, out_v,
    cols_s, count_s, leaf_src_s, par_src_s, top_src_s,
    leaf_t, par_t, top_t, par_w, near_acc, leaf_acc,
    x_sem, in_sem, near_sem, halo_send, halo_recv, own_sem,
    spread_send, spread_recv, across_send, across_recv, onward_send, onward_recv,
    opposite_send, opposite_recv, share_send, share_recv, out_sem,
):
    clus = lax.axis_index("clus")
    tree = lax.axis_index("leaf")
    y, x = lax.div(clus, 4), lax.rem(clus, 4)
    z, core = lax.div(tree, 2), lax.rem(tree, 2)

    def device(dz=0, dc=0, dy=0, dx=0):
        return (
            lax.rem(y + dy, 4) * 4 + lax.rem(x + dx, 4),
            lax.rem(z + dz, 4) * 2 + lax.rem(core + dc, 2),
        )

    ta, tb, tc = x + core * (y - x), y + core * (z - y), z + core * (x - z)

    right, left = (lax.rem(clus + 1, 16), tree), (lax.rem(clus + 15, 16), tree)
    sibling = device(dc=1)
    along = {
        "z": [device(dz=d) for d in (1, 2, 3)],
        "y": [device(dy=d) for d in (1, 2, 3)],
        "x": [device(dx=d) for d in (1, 2, 3)],
    }
    partners = [right, left, sibling] + along["z"] + along["y"] + along["x"]
    barrier = pltpu.get_barrier_semaphore()
    for partner in partners:
        pl.semaphore_signal(barrier, inc=1, device_id=partner, device_id_type=pl.DeviceIdType.MESH)

    def fetch(i, src, dst):
        return pltpu.make_async_copy(src, dst, in_sem.at[i])

    def x_fetch(g):
        return pltpu.make_async_copy(rhs.at[:, pl.ds(g * PTS, PTS)], x_own.at[g], x_sem)

    for g in range(LEAVES):
        x_fetch(g).start()
    fetches = [
        fetch(1, basis, basis_v),
        fetch(2, lt, lt_v),
        fetch(3, pt, pt_v),
        fetch(4, cols, cols_s),
        fetch(5, count, count_s),
        fetch(6, leaf_src, leaf_src_s),
        fetch(7, par_src, par_src_s),
        fetch(8, top_src, top_src_s),
        fetch(9, par_coup, par_coup_v),
        fetch(10, leaf_coup, leaf_coup_v),
        fetch(11, top_coup, top_coup_v),
    ]
    for f in fetches[:3]:
        f.start()

    def near_fetch(i):
        pair = pl.ds(2 * i, 2)
        return pltpu.make_async_copy(near.at[pair], near_v.at[pair], near_sem.at[i])

    for f in fetches[3:8]:
        f.start()

    def near_fetches(lo, hi):
        @pl.loop(lo, hi)
        def _(i):
            near_fetch(i).start()

    near_fetches(4, 8)
    for f in fetches[8:]:
        f.start()
    near_fetches(8, 12)
    near_fetches(0, 4)


    def remote(src, dst, send, recv, to):
        return pltpu.make_async_remote_copy(
            src_ref=src, dst_ref=dst, send_sem=send, recv_sem=recv, device_id=to,
            device_id_type=pl.DeviceIdType.MESH,
        )

    x_v[ZERO] = jnp.zeros((32, PTS), BF16)
    x_own[LEAVES] = jnp.zeros((32, PTS), BF16)
    def leaf_columns(g):
        return rhs.at[:, pl.ds(g * PTS, PTS)]

    x_halos = [
        remote(x_own.at[pl.ds(LEAVES - HALO, HALO)], x_v.at[pl.ds(0, HALO)], halo_send.at[0], halo_recv.at[0], right),
        remote(x_own.at[pl.ds(0, HALO)], x_v.at[pl.ds(LEAVES + HALO, HALO)], halo_send.at[0], halo_recv.at[0], left),
    ]
    leaf_halos = [
        remote(leaf_t.at[pl.ds(LEAVES, HALO)], leaf_t.at[pl.ds(0, HALO)], halo_send.at[1], halo_recv.at[1], right),
        remote(leaf_t.at[pl.ds(HALO, HALO)], leaf_t.at[pl.ds(LEAVES + HALO, HALO)], halo_send.at[1], halo_recv.at[1], left),
    ]

    def halo_wait(i, table):
        both = table.at[pl.ds(0, 2 * HALO)]
        remote(both, both, halo_send.at[i], halo_recv.at[i], right).wait()

    own = x_own.at[pl.ds(0, LEAVES)]
    pltpu.make_async_copy(own, own, x_sem).wait()
    own_copy = pltpu.make_async_copy(x_own.at[pl.ds(0, LEAVES)], x_v.at[pl.ds(HALO, LEAVES)], own_sem)
    own_copy.start()
    for f in fetches[:2]:
        f.wait()

    def unit(part):
        if part == TOP:
            return top_t.at[core, tc, tb, ta]
        return par_t.at[z, core, y, x, pl.ds(2 * part, 2)]

    def row(part, r, d):
        if part == TOP:
            return top_t.at[core, lax.rem(tc + 4 - d, 4), lax.rem(tb + 4 - r, 4)]
        a, b, c = ORDERS[part]
        at = {"z": z, "y": y, "x": x}
        at[b], at[c] = lax.rem(at[b] + 4 - r, 4), lax.rem(at[c] + 4 - d, 4)
        at[a] = slice(None)
        return par_t.at[at["z"], core, at["y"], at["x"], pl.ds(2 * part, 2)]

    def target(part, axis, d):
        if part == TOP:
            one, two = ("xyz"[axis], "yzx"[axis])
            return device(**{"d" + one: d * (1 - core), "d" + two: d * core})
        return along[ORDERS[part][axis]][d - 1]

    def spread(part, k):
        return remote(unit(part), unit(part), spread_send, spread_recv, target(part, 0, k + 1))

    def across(part, k):
        ref = row(part, 0, 0)
        return remote(ref, ref, across_send, across_recv.at[k], target(part, 1, k + 1))

    def onward(part, r, way):
        ref = row(part, r, 0)
        return remote(ref, ref, onward_send, onward_recv.at[r], target(part, 2, (1, 3)[way]))

    def opposite(part, r):
        ref = row(part, r, 0)
        return remote(ref, ref, opposite_send, opposite_recv.at[r], target(part, 2, 2))

    def share(part, r, d):
        ref = row(part, r, d)
        return remote(ref, ref, share_send, share_recv.at[int(part == TOP)], sibling)

    all_parents = par_t.reshape(768, 16, 128)

    def await_tiles(semaphore, n):
        ref = all_parents.at[pl.ds(0, n)]
        pltpu.make_async_copy(ref, ref, semaphore).wait()

    for g in range(LEAVES):
        leaf_t[HALO + g] = pack(dot_t(x_own[g], basis_v[g]))
    pl.semaphore_wait(barrier, len(partners))
    for c in leaf_halos:
        c.start()
    parent_tiles = []
    for p in range(PARENTS):
        lhs = side_by_side([leaf_t[HALO + 4 * p + c] for c in range(4)])
        tile = pack(dot(lhs, lt_v[4 * p:4 * p + 4].reshape(256, 64)))
        parent_tiles.append(tile)
        par_t[z, core, y, x, p] = tile
        if p % 2:
            for k in (1, 0, 2):
                spread(p // 2, k).start()

    fetches[2].wait()
    lhs = side_by_side(parent_tiles)
    top_t[core, tc, tb, ta] = pack(dot(lhs, pt_v[...].reshape(PARENTS * 64, 64)))
    for k in (1, 0, 2):
        spread(TOP, k).start()
    for c in x_halos:
        c.start()

    def pack_weights(q, present):
        nothing = jnp.zeros((64, 64), BF16)
        for h in range(2):
            for k in range(4):
                blocks = [par_coup_v[3 * h + n, 4 * q + k] if k < present else nothing for n in range(3)]
                par_w[h, q, 64 * k:64 * k + 64] = jnp.concatenate(blocks + [nothing], axis=1)

    first = clus * LEAVES - HALO

    def near_leaf(g, table, first, end):
        total = None
        for n in range(NEAR):
            live = jnp.clip(count_s[0, g] - n, 0, 1)
            at = end + live * (jnp.clip(cols_s[n, 0, g] - first, 0, end - 1) - end)
            term = dot(table[at], near_v[g, n])
            total = term if total is None else total + term
        near_acc[g] = total

    for f in fetches[3:8]:
        f.wait()

    def near_inner(lo, hi):
        @pl.loop(lo, hi)
        def _(i):
            near_fetch(i).wait()
            for g in (2 * i, 2 * i + 1):
                near_leaf(g, x_own, clus * LEAVES, LEAVES)

    def near_outer(lo, hi):
        @pl.loop(lo, hi)
        def _(i):
            near_fetch(i).wait()
            for g in (2 * i, 2 * i + 1):
                near_leaf(g, x_v, first, ZERO)

    near_inner(4, 8)
    await_tiles(spread_recv, 3 * 7)
    for part in ALL:
        for k in (0, 2, 1):
            across(part, k).start()
        for way in (0, 1):
            onward(part, 0, way).start()
        opposite(part, 0).start()
        share(part, 0, 0).start()
    fetches[8].wait()

    @pl.loop(0, QUADS - 1)
    def _(q):
        pack_weights(q, 4)

    pack_weights(QUADS - 1, 3)
    halo_wait(1, leaf_t)
    fetches[9].wait()

    @pl.loop(0, PARENTS)
    def _(p):
        fields = []
        for c in range(4):
            g = 4 * p + c
            total = None
            for half in range(2):
                tiles = []
                for j in range(4 * half, 4 * half + 4):
                    tiles.append(leaf_t[jnp.clip(leaf_src_s[j, g] - first, 0, ZERO - 1)])
                term = dot(side_by_side(tiles), leaf_coup_v[g, 4 * half:4 * half + 4].reshape(256, 64))
                total = term if total is None else total + term
            fields.append(total)
        leaf_acc[p] = jnp.concatenate(fields, axis=1)

    for r in (1, 3, 2):
        await_tiles(across_recv.at[r - 1], 4 * 7)
        for part in ALL:
            for way in (0, 1):
                onward(part, r, way).start()
            opposite(part, r).start()
            share(part, r, 0).start()
    own_copy.wait()
    halo_wait(0, x_v)
    near_outer(8, 10)
    for r in (0, 1, 3, 2):
        await_tiles(onward_recv.at[r], 8 * 7)
        for part in ALL:
            share(part, r, 1).start()
            share(part, r, 3).start()
        if r == 0:
            near_outer(10, 12)
        if r == 1:
            near_outer(0, 2)
        if r == 3:
            near_outer(2, 4)
        await_tiles(opposite_recv.at[r], 4 * 7)
        for part in ALL:
            share(part, r, 2).start()

    await_tiles(share_recv.at[1], 64)

    fetches[10].wait()
    total = None
    for j in range(0, 27, 4):
        tiles = []
        for i in range(j, min(j + 4, 27)):
            t = top_src_s[0, 0, i]
            tz, tcore, ty, tx = t >> 5, (t >> 4) & 1, (t >> 2) & 3, t & 3
            tiles.append(top_t[tcore, tz + tcore * (tx - tz), ty + tcore * (tz - ty), tx + tcore * (ty - tx)])
        weights = top_coup_v[j:j + len(tiles)].reshape(len(tiles) * 64, 64)
        term = dot(side_by_side(tiles)[:, :len(tiles) * 64], weights)
        total = term if total is None else total + term
    top_field = total.astype(BF16)
    await_tiles(share_recv.at[0], 384)
    top_down = dot_t(top_field, pt_v[...].reshape(PARENTS * 64, 64))
    lane = lax.broadcasted_iota(jnp.int32, (32, 256), 1) // 64
    sums = []
    for h in range(2):
        total = None
        for q in range(QUADS):
            lhs = []
            for p in range(3 * h, 3 * h + 3):
                lhs.append(side_by_side([all_parents[par_src_s[p, 0, i]] for i in range(4 * q, min(4 * q + 4, 27))]))
            term = dot(jnp.concatenate(lhs, axis=0), par_w[h, q])
            total = term if total is None else total + term
        sums += [total[32 * n:32 * n + 32, 64 * n:64 * n + 64] for n in range(3)]
    for p in range(PARENTS):
        total = sums[p] + top_down[:, 64 * p:64 * p + 64]
        field = leaf_acc[p] + dot_t(total.astype(BF16), lt_v[4 * p:4 * p + 4].reshape(256, 64))
        field = field.astype(BF16)
        masked = jnp.concatenate(
            [jnp.where(lane == c, field, jnp.zeros_like(field)) for c in range(4)], axis=0
        )
        far = dot(masked, basis_v[4 * p:4 * p + 4].reshape(256, 256))
        for c in range(4):
            g = 4 * p + c
            out_v[:, g * PTS:(g + 1) * PTS] = (near_acc[g] + far[32 * c:32 * c + 32]).astype(BF16)
        columns = pl.ds(4 * p * PTS, 4 * PTS)
        pltpu.make_async_copy(out_v.at[:, columns], out.at[:, columns], out_sem).start()

    await_tiles(spread_send, 3 * 7)
    await_tiles(across_send, 12 * 7)
    await_tiles(onward_send, 32 * 7)
    await_tiles(opposite_send, 16 * 7)
    await_tiles(share_send, 64 * 7)
    pltpu.make_async_copy(out_v, out_v, out_sem).wait()


def local(
    right_sides, near_blocks, near_cols, near_count, basis, leaf_transfer, par_transfer,
    leaf_src, leaf_coup, par_src, par_coup, top_src, top_coup,
):
    vma = pltpu.VMEM
    call = pl.pallas_call(
        kernel,
        out_shape=jax.ShapeDtypeStruct((32, LEAVES * PTS), BF16),
        in_specs=[pl.BlockSpec(memory_space=pl.ANY)] * 13,
        out_specs=pl.BlockSpec(memory_space=pl.ANY),
        scratch_shapes=[
            vma((LEAVES + 1, 32, PTS), BF16),
            vma((ZERO + 1, 32, PTS), BF16),
            vma((LEAVES, NEAR, PTS, PTS), BF16),
            vma((LEAVES, 64, PTS), BF16),
            vma((LEAVES, 64, 64), BF16),
            vma((PARENTS, 64, 64), BF16),
            vma((LEAVES, 8, 64, 64), BF16),
            vma((PARENTS, 27, 64, 64), BF16),
            vma((27, 64, 64), BF16),
            vma((32, LEAVES * PTS), BF16),
            pltpu.SMEM((NEAR, 1, LEAVES), jnp.int32),
            pltpu.SMEM((1, LEAVES), jnp.int32),
            pltpu.SMEM((8, LEAVES), jnp.int32),
            pltpu.SMEM((PARENTS, 1, 27), jnp.int32),
            pltpu.SMEM((1, 1, 27), jnp.int32),
            vma((LEAVES + 2 * HALO, 16, 128), BF16),
            vma((4, 2, 4, 4, PARENTS, 16, 128), BF16),
            vma((2, 4, 4, 4, 16, 128), BF16),
            vma((2, QUADS, 256, 256), BF16),
            vma((LEAVES, 32, PTS), F32),
            vma((PARENTS, 32, PTS), F32),
            pltpu.SemaphoreType.DMA,
            pltpu.SemaphoreType.DMA((12,)),
            pltpu.SemaphoreType.DMA((LEAVES // 2,)),
            pltpu.SemaphoreType.DMA((2,)),
            pltpu.SemaphoreType.DMA((2,)),
            pltpu.SemaphoreType.DMA,
            pltpu.SemaphoreType.DMA,
            pltpu.SemaphoreType.DMA,
            pltpu.SemaphoreType.DMA,
            pltpu.SemaphoreType.DMA((3,)),
            pltpu.SemaphoreType.DMA,
            pltpu.SemaphoreType.DMA((4,)),
            pltpu.SemaphoreType.DMA,
            pltpu.SemaphoreType.DMA((4,)),
            pltpu.SemaphoreType.DMA,
            pltpu.SemaphoreType.DMA((2,)),
            pltpu.SemaphoreType.DMA,
        ],
        compiler_params=pltpu.CompilerParams(
            collective_id=0, has_side_effects=True, vmem_limit_bytes=63 * 2**20
        ),
    )
    out = call(
        right_sides[:, 0],
        near_blocks[0],
        jnp.transpose(near_cols, (2, 0, 1)),
        near_count,
        jnp.swapaxes(basis[0], 1, 2),
        leaf_transfer[0],
        par_transfer[0],
        jnp.transpose(leaf_src[0], (1, 0)),
        leaf_coup[0],
        jnp.transpose(par_src, (1, 0, 2)),
        par_coup[0],
        top_src,
        top_coup[0, 0],
    )
    return out[:, None, :]


def solution(mesh):
    return jax.shard_map(
        local,
        mesh=mesh,
        in_specs=(
            P(None, "leaf", "clus"),
            P("leaf", "clus", None, None, None),
            P("leaf", "clus", None),
            P("leaf", "clus"),
            P("leaf", "clus", None, None),
            P("leaf", "clus", None, None),
            P("leaf", "clus", None, None),
            P("leaf", "clus", None),
            P("leaf", "clus", None, None, None),
            P("leaf", "clus", None),
            P("leaf", "clus", None, None, None),
            P("leaf", "clus", None),
            P("leaf", "clus", None, None, None),
        ),
        out_specs=P(None, "leaf", "clus"),
        check_vma=False,
    )
```

```python
import jax
import jax.numpy as jnp
from jax import lax
from jax.experimental import pallas as pl
from jax.experimental.pallas import tpu as pltpu
from jax.sharding import PartitionSpec as P

F32 = jnp.float32
BF16 = jnp.bfloat16
LEAVES = 24
PARENTS = 6
HALO = 8
NEAR = 5
PTS = 256
ZERO = LEAVES + 2 * HALO
ORDERS = ("xyz", "yzx", "zxy")
ALL = (3, 0, 1, 2)
TILES = (2, 2, 2, 1)
QUADS = 7
TOP = 3


def dot(a, b):
    return lax.dot_general(a, b, (((1,), (0,)), ((), ())), preferred_element_type=F32)


def dot_t(a, b):
    return lax.dot_general(a, b, (((1,), (1,)), ((), ())), preferred_element_type=F32)


def pack(y):
    return jnp.concatenate([y[:16], y[16:]], axis=1).astype(BF16)


def side_by_side(tiles):
    low = lax.broadcasted_iota(jnp.int32, (16, 128), 1) < 64
    columns = []
    for i in range(0, len(tiles), 2):
        a = tiles[i].astype(F32)
        b = tiles[i + 1].astype(F32) if i + 1 < len(tiles) else jnp.zeros_like(a)
        top = jnp.where(low, a, pltpu.roll(b, 64, 1))
        bottom = jnp.where(low, pltpu.roll(a, 64, 1), b)
        columns.append(jnp.concatenate([top, bottom], axis=0).astype(BF16))
    return jnp.concatenate(columns, axis=1)


def kernel(
    rhs, near, cols, count, basis, lt, pt, leaf_src, leaf_coup, par_src, par_coup, top_src, top_coup,
    out,
    x_own, x_v, near_v, basis_v, lt_v, pt_v, leaf_coup_v, par_coup_v, top_coup_v, out_v,
    cols_s, count_s, leaf_src_s, par_src_s, top_src_s,
    leaf_t, par_t, top_t, par_w, near_acc, leaf_acc,
    x_sem, in_sem, near_sem, halo_send, halo_recv, own_sem,
    spread_send, spread_recv, across_send, across_recv, onward_send, onward_recv,
    opposite_send, opposite_recv, share_send, share_recv, out_sem,
):
    clus = lax.axis_index("clus")
    tree = lax.axis_index("leaf")
    y, x = lax.div(clus, 4), lax.rem(clus, 4)
    z, core = lax.div(tree, 2), lax.rem(tree, 2)

    def device(dz=0, dc=0, dy=0, dx=0):
        return (
            lax.rem(y + dy, 4) * 4 + lax.rem(x + dx, 4),
            lax.rem(z + dz, 4) * 2 + lax.rem(core + dc, 2),
        )

    ta, tb, tc = x + core * (y - x), y + core * (z - y), z + core * (x - z)

    right, left = (lax.rem(clus + 1, 16), tree), (lax.rem(clus + 15, 16), tree)
    sibling = device(dc=1)
    along = {
        "z": [device(dz=d) for d in (1, 2, 3)],
        "y": [device(dy=d) for d in (1, 2, 3)],
        "x": [device(dx=d) for d in (1, 2, 3)],
    }
    partners = [right, left, sibling] + along["z"] + along["y"] + along["x"]
    barrier = pltpu.get_barrier_semaphore()
    for partner in partners:
        pl.semaphore_signal(barrier, inc=1, device_id=partner, device_id_type=pl.DeviceIdType.MESH)

    def fetch(i, src, dst):
        return pltpu.make_async_copy(src, dst, in_sem.at[i])

    def x_fetch(g):
        return pltpu.make_async_copy(rhs.at[:, pl.ds(g * PTS, PTS)], x_own.at[g], x_sem)

    for g in range(LEAVES):
        x_fetch(g).start()
    fetches = [
        fetch(1, basis, basis_v),
        fetch(2, lt, lt_v),
        fetch(3, pt, pt_v),
        fetch(4, cols, cols_s),
        fetch(5, count, count_s),
        fetch(6, leaf_src, leaf_src_s),
        fetch(7, par_src, par_src_s),
        fetch(8, top_src, top_src_s),
        fetch(9, par_coup, par_coup_v),
        fetch(10, leaf_coup, leaf_coup_v),
        fetch(11, top_coup, top_coup_v),
    ]
    for f in fetches[:3]:
        f.start()

    def near_fetch(i):
        pair = pl.ds(2 * i, 2)
        return pltpu.make_async_copy(near.at[pair], near_v.at[pair], near_sem.at[i])

    for f in fetches[3:8]:
        f.start()

    def near_fetches(lo, hi):
        @pl.loop(lo, hi)
        def _(i):
            near_fetch(i).start()

    near_fetches(4, 8)
    for f in fetches[8:]:
        f.start()
    near_fetches(8, 12)
    near_fetches(0, 4)


    def remote(src, dst, send, recv, to):
        return pltpu.make_async_remote_copy(
            src_ref=src, dst_ref=dst, send_sem=send, recv_sem=recv, device_id=to,
            device_id_type=pl.DeviceIdType.MESH,
        )

    x_v[ZERO] = jnp.zeros((32, PTS), BF16)
    x_own[LEAVES] = jnp.zeros((32, PTS), BF16)

    x_halos = [
        remote(x_own.at[pl.ds(LEAVES - HALO, HALO)], x_v.at[pl.ds(0, HALO)], halo_send.at[0], halo_recv.at[0], right),
        remote(x_own.at[pl.ds(0, HALO)], x_v.at[pl.ds(LEAVES + HALO, HALO)], halo_send.at[0], halo_recv.at[0], left),
    ]
    leaf_halos = [
        remote(leaf_t.at[pl.ds(LEAVES, HALO)], leaf_t.at[pl.ds(0, HALO)], halo_send.at[1], halo_recv.at[1], right),
        remote(leaf_t.at[pl.ds(HALO, HALO)], leaf_t.at[pl.ds(LEAVES + HALO, HALO)], halo_send.at[1], halo_recv.at[1], left),
    ]

    def halo_wait(i, table):
        both = table.at[pl.ds(0, 2 * HALO)]
        remote(both, both, halo_send.at[i], halo_recv.at[i], right).wait()

    own = x_own.at[pl.ds(0, LEAVES)]
    pltpu.make_async_copy(own, own, x_sem).wait()
    own_copy = pltpu.make_async_copy(x_own.at[pl.ds(0, LEAVES)], x_v.at[pl.ds(HALO, LEAVES)], own_sem)
    own_copy.start()
    for f in fetches[:2]:
        f.wait()

    def unit(part):
        if part == TOP:
            return top_t.at[core, tc, tb, ta]
        return par_t.at[z, core, y, x, pl.ds(2 * part, 2)]

    def row(part, r, d):
        if part == TOP:
            return top_t.at[core, lax.rem(tc + 4 - d, 4), lax.rem(tb + 4 - r, 4)]
        a, b, c = ORDERS[part]
        at = {"z": z, "y": y, "x": x}
        at[b], at[c] = lax.rem(at[b] + 4 - r, 4), lax.rem(at[c] + 4 - d, 4)
        at[a] = slice(None)
        return par_t.at[at["z"], core, at["y"], at["x"], pl.ds(2 * part, 2)]

    def target(part, axis, d):
        if part == TOP:
            one, two = ("xyz"[axis], "yzx"[axis])
            return device(**{"d" + one: d * (1 - core), "d" + two: d * core})
        return along[ORDERS[part][axis]][d - 1]

    def spread(part, k):
        return remote(unit(part), unit(part), spread_send, spread_recv.at[part], target(part, 0, k + 1))

    def across(part, k):
        ref = row(part, 0, 0)
        return remote(ref, ref, across_send, across_recv.at[4 * k + part], target(part, 1, k + 1))

    def onward(part, r, way):
        ref = row(part, r, 0)
        return remote(ref, ref, onward_send, onward_recv.at[r], target(part, 2, (1, 3)[way]))

    def opposite(part, r):
        ref = row(part, r, 0)
        return remote(ref, ref, opposite_send, opposite_recv.at[r], target(part, 2, 2))

    def share(part, r, d):
        ref = row(part, r, d)
        return remote(ref, ref, share_send, share_recv.at[int(part == TOP)], sibling)

    all_parents = par_t.reshape(768, 16, 128)

    def await_tiles(semaphore, n):
        ref = all_parents.at[pl.ds(0, n)]
        pltpu.make_async_copy(ref, ref, semaphore).wait()

    for g in range(LEAVES):
        leaf_t[HALO + g] = pack(dot_t(x_own[g], basis_v[g]))
    pl.semaphore_wait(barrier, len(partners))
    for c in leaf_halos:
        c.start()
    parent_tiles = []
    for p in range(PARENTS):
        lhs = side_by_side([leaf_t[HALO + 4 * p + c] for c in range(4)])
        tile = pack(dot(lhs, lt_v[4 * p:4 * p + 4].reshape(256, 64)))
        parent_tiles.append(tile)
        par_t[z, core, y, x, p] = tile
        if p % 2:
            for k in (1, 0, 2):
                spread(p // 2, k).start()

    fetches[2].wait()
    lhs = side_by_side(parent_tiles)
    top_t[core, tc, tb, ta] = pack(dot(lhs, pt_v[...].reshape(PARENTS * 64, 64)))
    for k in (1, 0, 2):
        spread(TOP, k).start()
    for c in x_halos:
        c.start()

    def pack_weights(q, present):
        nothing = jnp.zeros((64, 64), BF16)
        for h in range(2):
            for k in range(4):
                blocks = [par_coup_v[3 * h + n, 4 * q + k] if k < present else nothing for n in range(3)]
                par_w[h, q, 64 * k:64 * k + 64] = jnp.concatenate(blocks + [nothing], axis=1)

    first = clus * LEAVES - HALO

    def near_leaf(g, table, first, end):
        total = None
        for n in range(NEAR):
            live = jnp.clip(count_s[0, g] - n, 0, 1)
            at = end + live * (jnp.clip(cols_s[n, 0, g] - first, 0, end - 1) - end)
            term = dot(table[at], near_v[g, n])
            total = term if total is None else total + term
        near_acc[g] = total

    for f in fetches[3:8]:
        f.wait()

    def near_inner(lo, hi):
        @pl.loop(lo, hi)
        def _(i):
            near_fetch(i).wait()
            for g in (2 * i, 2 * i + 1):
                near_leaf(g, x_own, clus * LEAVES, LEAVES)

    def near_outer(lo, hi):
        @pl.loop(lo, hi)
        def _(i):
            near_fetch(i).wait()
            for g in (2 * i, 2 * i + 1):
                near_leaf(g, x_v, first, ZERO)

    near_inner(4, 8)
    for part in ALL:
        await_tiles(spread_recv.at[part], 3 * TILES[part])
        for k in (0, 2, 1):
            across(part, k).start()
        for way in (0, 1):
            onward(part, 0, way).start()
        opposite(part, 0).start()
        share(part, 0, 0).start()
    fetches[8].wait()

    @pl.loop(0, QUADS - 1)
    def _(q):
        pack_weights(q, 4)

    pack_weights(QUADS - 1, 3)
    halo_wait(1, leaf_t)
    fetches[9].wait()

    @pl.loop(0, PARENTS)
    def _(p):
        fields = []
        for c in range(4):
            g = 4 * p + c
            total = None
            for half in range(2):
                tiles = []
                for j in range(4 * half, 4 * half + 4):
                    tiles.append(leaf_t[jnp.clip(leaf_src_s[j, g] - first, 0, ZERO - 1)])
                term = dot(side_by_side(tiles), leaf_coup_v[g, 4 * half:4 * half + 4].reshape(256, 64))
                total = term if total is None else total + term
            fields.append(total)
        leaf_acc[p] = jnp.concatenate(fields, axis=1)

    for r in (3, 1, 2):
        for part in ALL:
            await_tiles(across_recv.at[4 * (r - 1) + part], 4 * TILES[part])
            for way in (0, 1):
                onward(part, r, way).start()
            opposite(part, r).start()
            share(part, r, 0).start()
    own_copy.wait()
    halo_wait(0, x_v)
    near_outer(8, 10)
    for r in (0, 3, 1, 2):
        await_tiles(onward_recv.at[r], 8 * 7)
        for part in ALL:
            share(part, r, 1).start()
            share(part, r, 3).start()
        if r == 0:
            near_outer(10, 12)
        if r == 3:
            near_outer(0, 2)
        if r == 1:
            near_outer(2, 4)
        await_tiles(opposite_recv.at[r], 4 * 7)
        for part in ALL:
            share(part, r, 2).start()

    await_tiles(share_recv.at[1], 64)

    fetches[10].wait()
    total = None
    for j in range(0, 27, 4):
        tiles = []
        for i in range(j, min(j + 4, 27)):
            t = top_src_s[0, 0, i]
            tz, tcore, ty, tx = t >> 5, (t >> 4) & 1, (t >> 2) & 3, t & 3
            tiles.append(top_t[tcore, tz + tcore * (tx - tz), ty + tcore * (tz - ty), tx + tcore * (ty - tx)])
        weights = top_coup_v[j:j + len(tiles)].reshape(len(tiles) * 64, 64)
        term = dot(side_by_side(tiles)[:, :len(tiles) * 64], weights)
        total = term if total is None else total + term
    top_field = total.astype(BF16)
    await_tiles(share_recv.at[0], 384)
    top_down = dot_t(top_field, pt_v[...].reshape(PARENTS * 64, 64))
    lane = lax.broadcasted_iota(jnp.int32, (32, 256), 1) // 64
    sums = []
    for h in range(2):
        total = None
        for q in range(QUADS):
            lhs = []
            for p in range(3 * h, 3 * h + 3):
                lhs.append(side_by_side([all_parents[par_src_s[p, 0, i]] for i in range(4 * q, min(4 * q + 4, 27))]))
            term = dot(jnp.concatenate(lhs, axis=0), par_w[h, q])
            total = term if total is None else total + term
        sums += [total[32 * n:32 * n + 32, 64 * n:64 * n + 64] for n in range(3)]
    for p in range(PARENTS):
        total = sums[p] + top_down[:, 64 * p:64 * p + 64]
        field = leaf_acc[p] + dot_t(total.astype(BF16), lt_v[4 * p:4 * p + 4].reshape(256, 64))
        field = field.astype(BF16)
        masked = jnp.concatenate(
            [jnp.where(lane == c, field, jnp.zeros_like(field)) for c in range(4)], axis=0
        )
        far = dot(masked, basis_v[4 * p:4 * p + 4].reshape(256, 256))
        for c in range(4):
            g = 4 * p + c
            out_v[:, g * PTS:(g + 1) * PTS] = (near_acc[g] + far[32 * c:32 * c + 32]).astype(BF16)
        columns = pl.ds(4 * p * PTS, 4 * PTS)
        pltpu.make_async_copy(out_v.at[:, columns], out.at[:, columns], out_sem).start()

    await_tiles(spread_send, 3 * 7)
    await_tiles(across_send, 12 * 7)
    await_tiles(onward_send, 32 * 7)
    await_tiles(opposite_send, 16 * 7)
    await_tiles(share_send, 64 * 7)
    pltpu.make_async_copy(out_v, out_v, out_sem).wait()


def local(
    right_sides, near_blocks, near_cols, near_count, basis, leaf_transfer, par_transfer,
    leaf_src, leaf_coup, par_src, par_coup, top_src, top_coup,
):
    vma = pltpu.VMEM
    call = pl.pallas_call(
        kernel,
        out_shape=jax.ShapeDtypeStruct((32, LEAVES * PTS), BF16),
        in_specs=[pl.BlockSpec(memory_space=pl.ANY)] * 13,
        out_specs=pl.BlockSpec(memory_space=pl.ANY),
        scratch_shapes=[
            vma((LEAVES + 1, 32, PTS), BF16),
            vma((ZERO + 1, 32, PTS), BF16),
            vma((LEAVES, NEAR, PTS, PTS), BF16),
            vma((LEAVES, 64, PTS), BF16),
            vma((LEAVES, 64, 64), BF16),
            vma((PARENTS, 64, 64), BF16),
            vma((LEAVES, 8, 64, 64), BF16),
            vma((PARENTS, 27, 64, 64), BF16),
            vma((27, 64, 64), BF16),
            vma((32, LEAVES * PTS), BF16),
            pltpu.SMEM((NEAR, 1, LEAVES), jnp.int32),
            pltpu.SMEM((1, LEAVES), jnp.int32),
            pltpu.SMEM((8, LEAVES), jnp.int32),
            pltpu.SMEM((PARENTS, 1, 27), jnp.int32),
            pltpu.SMEM((1, 1, 27), jnp.int32),
            vma((LEAVES + 2 * HALO, 16, 128), BF16),
            vma((4, 2, 4, 4, PARENTS, 16, 128), BF16),
            vma((2, 4, 4, 4, 16, 128), BF16),
            vma((2, QUADS, 256, 256), BF16),
            vma((LEAVES, 32, PTS), F32),
            vma((PARENTS, 32, PTS), F32),
            pltpu.SemaphoreType.DMA,
            pltpu.SemaphoreType.DMA((12,)),
            pltpu.SemaphoreType.DMA((LEAVES // 2,)),
            pltpu.SemaphoreType.DMA((2,)),
            pltpu.SemaphoreType.DMA((2,)),
            pltpu.SemaphoreType.DMA,
            pltpu.SemaphoreType.DMA,
            pltpu.SemaphoreType.DMA((4,)),
            pltpu.SemaphoreType.DMA,
            pltpu.SemaphoreType.DMA((12,)),
            pltpu.SemaphoreType.DMA,
            pltpu.SemaphoreType.DMA((4,)),
            pltpu.SemaphoreType.DMA,
            pltpu.SemaphoreType.DMA((4,)),
            pltpu.SemaphoreType.DMA,
            pltpu.SemaphoreType.DMA((2,)),
            pltpu.SemaphoreType.DMA,
        ],
        compiler_params=pltpu.CompilerParams(
            collective_id=0, has_side_effects=True, vmem_limit_bytes=63 * 2**20
        ),
    )
    out = call(
        right_sides[:, 0],
        near_blocks[0],
        jnp.transpose(near_cols, (2, 0, 1)),
        near_count,
        jnp.swapaxes(basis[0], 1, 2),
        leaf_transfer[0],
        par_transfer[0],
        jnp.transpose(leaf_src[0], (1, 0)),
        leaf_coup[0],
        jnp.transpose(par_src, (1, 0, 2)),
        par_coup[0],
        top_src,
        top_coup[0, 0],
    )
    return out[:, None, :]


def solution(mesh):
    return jax.shard_map(
        local,
        mesh=mesh,
        in_specs=(
            P(None, "leaf", "clus"),
            P("leaf", "clus", None, None, None),
            P("leaf", "clus", None),
            P("leaf", "clus"),
            P("leaf", "clus", None, None),
            P("leaf", "clus", None, None),
            P("leaf", "clus", None, None),
            P("leaf", "clus", None),
            P("leaf", "clus", None, None, None),
            P("leaf", "clus", None),
            P("leaf", "clus", None, None, None),
            P("leaf", "clus", None),
            P("leaf", "clus", None, None, None),
        ),
        out_specs=P(None, "leaf", "clus"),
        check_vma=False,
    )
```

```python
import jax
import jax.numpy as jnp
from jax import lax
from jax.experimental import pallas as pl
from jax.experimental.pallas import tpu as pltpu
from jax.sharding import PartitionSpec as P

F32 = jnp.float32
BF16 = jnp.bfloat16
LEAVES = 24
PARENTS = 6
HALO = 8
NEAR = 5
PTS = 256
ZERO = LEAVES + 2 * HALO
ORDERS = ("xyz", "yzx", "zxy")
ALL = (3, 0, 1, 2)
TILES = (2, 2, 2, 1)
QUADS = 7
TOP = 3


def dot(a, b):
    return lax.dot_general(a, b, (((1,), (0,)), ((), ())), preferred_element_type=F32)


def dot_t(a, b):
    return lax.dot_general(a, b, (((1,), (1,)), ((), ())), preferred_element_type=F32)


def pack(y):
    return jnp.concatenate([y[:16], y[16:]], axis=1).astype(BF16)


def side_by_side(tiles):
    low = lax.broadcasted_iota(jnp.int32, (16, 128), 1) < 64
    columns = []
    for i in range(0, len(tiles), 2):
        a = tiles[i].astype(F32)
        b = tiles[i + 1].astype(F32) if i + 1 < len(tiles) else jnp.zeros_like(a)
        top = jnp.where(low, a, pltpu.roll(b, 64, 1))
        bottom = jnp.where(low, pltpu.roll(a, 64, 1), b)
        columns.append(jnp.concatenate([top, bottom], axis=0).astype(BF16))
    return jnp.concatenate(columns, axis=1)


def kernel(
    rhs, near, cols, count, basis, lt, pt, leaf_src, leaf_coup, par_src, par_coup, top_src, top_coup,
    out,
    x_own, x_v, near_v, basis_v, lt_v, pt_v, leaf_coup_v, par_coup_v, top_coup_v, out_v,
    cols_s, count_s, leaf_src_s, par_src_s, top_src_s,
    leaf_t, par_t, top_t, par_w, near_acc, leaf_acc,
    x_sem, in_sem, near_sem, halo_send, halo_recv, own_sem,
    spread_send, spread_recv, across_send, across_recv, onward_send, onward_recv,
    opposite_send, opposite_recv, share_send, share_recv, out_sem,
):
    clus = lax.axis_index("clus")
    tree = lax.axis_index("leaf")
    y, x = lax.div(clus, 4), lax.rem(clus, 4)
    z, core = lax.div(tree, 2), lax.rem(tree, 2)

    def device(dz=0, dc=0, dy=0, dx=0):
        return (
            lax.rem(y + dy, 4) * 4 + lax.rem(x + dx, 4),
            lax.rem(z + dz, 4) * 2 + lax.rem(core + dc, 2),
        )

    ta, tb, tc = x + core * (y - x), y + core * (z - y), z + core * (x - z)

    right, left = (lax.rem(clus + 1, 16), tree), (lax.rem(clus + 15, 16), tree)
    sibling = device(dc=1)
    along = {
        "z": [device(dz=d) for d in (1, 2, 3)],
        "y": [device(dy=d) for d in (1, 2, 3)],
        "x": [device(dx=d) for d in (1, 2, 3)],
    }
    partners = [right, left, sibling] + along["z"] + along["y"] + along["x"]
    barrier = pltpu.get_barrier_semaphore()
    for partner in partners:
        pl.semaphore_signal(barrier, inc=1, device_id=partner, device_id_type=pl.DeviceIdType.MESH)

    def fetch(i, src, dst):
        return pltpu.make_async_copy(src, dst, in_sem.at[i])

    def x_fetch(g):
        return pltpu.make_async_copy(rhs.at[:, pl.ds(g * PTS, PTS)], x_own.at[g], x_sem)

    for g in range(LEAVES):
        x_fetch(g).start()
    fetches = [
        fetch(1, basis, basis_v),
        fetch(2, lt, lt_v),
        fetch(3, pt, pt_v),
        fetch(4, cols, cols_s),
        fetch(5, count, count_s),
        fetch(6, leaf_src, leaf_src_s),
        fetch(7, par_src, par_src_s),
        fetch(8, top_src, top_src_s),
        fetch(9, par_coup, par_coup_v),
        fetch(10, leaf_coup, leaf_coup_v),
        fetch(11, top_coup, top_coup_v),
    ]
    for f in fetches[:3]:
        f.start()

    def near_fetch(i):
        pair = pl.ds(2 * i, 2)
        return pltpu.make_async_copy(near.at[pair], near_v.at[pair], near_sem.at[i])

    for f in fetches[3:8]:
        f.start()

    def near_fetches(lo, hi):
        @pl.loop(lo, hi)
        def _(i):
            near_fetch(i).start()

    near_fetches(4, 8)
    for f in fetches[8:]:
        f.start()
    near_fetches(8, 12)
    near_fetches(0, 4)


    def remote(src, dst, send, recv, to):
        return pltpu.make_async_remote_copy(
            src_ref=src, dst_ref=dst, send_sem=send, recv_sem=recv, device_id=to,
            device_id_type=pl.DeviceIdType.MESH,
        )

    x_v[ZERO] = jnp.zeros((32, PTS), BF16)
    x_own[LEAVES] = jnp.zeros((32, PTS), BF16)

    x_halos = [
        remote(x_own.at[pl.ds(LEAVES - HALO, HALO)], x_v.at[pl.ds(0, HALO)], halo_send.at[0], halo_recv.at[0], right),
        remote(x_own.at[pl.ds(0, HALO)], x_v.at[pl.ds(LEAVES + HALO, HALO)], halo_send.at[0], halo_recv.at[0], left),
    ]
    leaf_halos = [
        remote(leaf_t.at[pl.ds(LEAVES, HALO)], leaf_t.at[pl.ds(0, HALO)], halo_send.at[1], halo_recv.at[1], right),
        remote(leaf_t.at[pl.ds(HALO, HALO)], leaf_t.at[pl.ds(LEAVES + HALO, HALO)], halo_send.at[1], halo_recv.at[1], left),
    ]

    def halo_wait(i, table):
        both = table.at[pl.ds(0, 2 * HALO)]
        remote(both, both, halo_send.at[i], halo_recv.at[i], right).wait()

    own = x_own.at[pl.ds(0, LEAVES)]
    pltpu.make_async_copy(own, own, x_sem).wait()
    own_copy = pltpu.make_async_copy(x_own.at[pl.ds(0, LEAVES)], x_v.at[pl.ds(HALO, LEAVES)], own_sem)
    own_copy.start()
    for f in fetches[:2]:
        f.wait()

    def unit(part):
        if part == TOP:
            return top_t.at[core, tc, tb, ta]
        return par_t.at[z, core, y, x, pl.ds(2 * part, 2)]

    def row(part, r, d):
        if part == TOP:
            return top_t.at[core, lax.rem(tc + 4 - d, 4), lax.rem(tb + 4 - r, 4)]
        a, b, c = ORDERS[part]
        at = {"z": z, "y": y, "x": x}
        at[b], at[c] = lax.rem(at[b] + 4 - r, 4), lax.rem(at[c] + 4 - d, 4)
        at[a] = slice(None)
        return par_t.at[at["z"], core, at["y"], at["x"], pl.ds(2 * part, 2)]

    def target(part, axis, d):
        if part == TOP:
            one, two = ("xyz"[axis], "yzx"[axis])
            return device(**{"d" + one: d * (1 - core), "d" + two: d * core})
        return along[ORDERS[part][axis]][d - 1]

    def spread(part, k):
        return remote(unit(part), unit(part), spread_send, spread_recv.at[part], target(part, 0, k + 1))

    def across(part, k):
        ref = row(part, 0, 0)
        return remote(ref, ref, across_send, across_recv.at[4 * k + part], target(part, 1, k + 1))

    def onward(part, r, way):
        ref = row(part, r, 0)
        return remote(ref, ref, onward_send, onward_recv.at[r], target(part, 2, (1, 3)[way]))

    def opposite(part, r):
        ref = row(part, r, 0)
        return remote(ref, ref, opposite_send, opposite_recv.at[r], target(part, 2, 2))

    def share(part, r, d):
        ref = row(part, r, d)
        return remote(ref, ref, share_send, share_recv.at[int(part == TOP)], sibling)

    all_parents = par_t.reshape(768, 16, 128)

    def await_tiles(semaphore, n):
        ref = all_parents.at[pl.ds(0, n)]
        pltpu.make_async_copy(ref, ref, semaphore).wait()

    for g in range(LEAVES):
        leaf_t[HALO + g] = pack(dot_t(x_own[g], basis_v[g]))
    pl.semaphore_wait(barrier, len(partners))
    for c in leaf_halos:
        c.start()
    parent_tiles = []
    for p in range(PARENTS):
        lhs = side_by_side([leaf_t[HALO + 4 * p + c] for c in range(4)])
        tile = pack(dot(lhs, lt_v[4 * p:4 * p + 4].reshape(256, 64)))
        parent_tiles.append(tile)
        par_t[z, core, y, x, p] = tile
        if p % 2:
            for k in (1, 0, 2):
                spread(p // 2, k).start()

    fetches[2].wait()
    lhs = side_by_side(parent_tiles)
    top_t[core, tc, tb, ta] = pack(dot(lhs, pt_v[...].reshape(PARENTS * 64, 64)))
    for k in (1, 0, 2):
        spread(TOP, k).start()
    for c in x_halos:
        c.start()

    def pack_weights(q, present):
        nothing = jnp.zeros((64, 64), BF16)
        for h in range(2):
            for k in range(4):
                blocks = [par_coup_v[3 * h + n, 4 * q + k] if k < present else nothing for n in range(3)]
                par_w[h, q, 64 * k:64 * k + 64] = jnp.concatenate(blocks + [nothing], axis=1)

    first = clus * LEAVES - HALO

    def near_leaf(g, table, first, end):
        total = None
        for n in range(NEAR):
            live = jnp.clip(count_s[0, g] - n, 0, 1)
            at = end + live * (jnp.clip(cols_s[n, 0, g] - first, 0, end - 1) - end)
            term = dot(table[at], near_v[g, n])
            total = term if total is None else total + term
        near_acc[g] = total

    for f in fetches[3:8]:
        f.wait()

    def near_inner(lo, hi):
        @pl.loop(lo, hi)
        def _(i):
            near_fetch(i).wait()
            for g in (2 * i, 2 * i + 1):
                near_leaf(g, x_own, clus * LEAVES, LEAVES)

    def near_outer(lo, hi):
        @pl.loop(lo, hi)
        def _(i):
            near_fetch(i).wait()
            for g in (2 * i, 2 * i + 1):
                near_leaf(g, x_v, first, ZERO)

    near_inner(4, 6)
    for part in ALL:
        await_tiles(spread_recv.at[part], 3 * TILES[part])
        for k in (0, 2, 1):
            across(part, k).start()
        for way in (0, 1):
            onward(part, 0, way).start()
        opposite(part, 0).start()
        share(part, 0, 0).start()
    near_inner(6, 8)
    fetches[8].wait()

    @pl.loop(0, QUADS - 1)
    def _(q):
        pack_weights(q, 4)

    pack_weights(QUADS - 1, 3)
    halo_wait(1, leaf_t)
    fetches[9].wait()

    @pl.loop(0, PARENTS)
    def _(p):
        fields = []
        for c in range(4):
            g = 4 * p + c
            total = None
            for half in range(2):
                tiles = []
                for j in range(4 * half, 4 * half + 4):
                    tiles.append(leaf_t[jnp.clip(leaf_src_s[j, g] - first, 0, ZERO - 1)])
                term = dot(side_by_side(tiles), leaf_coup_v[g, 4 * half:4 * half + 4].reshape(256, 64))
                total = term if total is None else total + term
            fields.append(total)
        leaf_acc[p] = jnp.concatenate(fields, axis=1)

    for r in (3, 1, 2):
        for part in ALL:
            await_tiles(across_recv.at[4 * (r - 1) + part], 4 * TILES[part])
            for way in (0, 1):
                onward(part, r, way).start()
            opposite(part, r).start()
            share(part, r, 0).start()
    own_copy.wait()
    halo_wait(0, x_v)
    near_outer(8, 10)
    for r in (0, 3, 1, 2):
        await_tiles(onward_recv.at[r], 8 * 7)
        for part in ALL:
            share(part, r, 1).start()
            share(part, r, 3).start()
        if r == 0:
            near_outer(10, 12)
        if r == 3:
            near_outer(0, 2)
        if r == 1:
            near_outer(2, 4)
        await_tiles(opposite_recv.at[r], 4 * 7)
        for part in ALL:
            share(part, r, 2).start()

    await_tiles(share_recv.at[1], 64)

    fetches[10].wait()
    total = None
    for j in range(0, 27, 4):
        tiles = []
        for i in range(j, min(j + 4, 27)):
            t = top_src_s[0, 0, i]
            tz, tcore, ty, tx = t >> 5, (t >> 4) & 1, (t >> 2) & 3, t & 3
            tiles.append(top_t[tcore, tz + tcore * (tx - tz), ty + tcore * (tz - ty), tx + tcore * (ty - tx)])
        weights = top_coup_v[j:j + len(tiles)].reshape(len(tiles) * 64, 64)
        term = dot(side_by_side(tiles)[:, :len(tiles) * 64], weights)
        total = term if total is None else total + term
    top_field = total.astype(BF16)
    await_tiles(share_recv.at[0], 384)
    top_down = dot_t(top_field, pt_v[...].reshape(PARENTS * 64, 64))
    lane = lax.broadcasted_iota(jnp.int32, (32, 256), 1) // 64
    sums = []
    for h in range(2):
        total = None
        for q in range(QUADS):
            lhs = []
            for p in range(3 * h, 3 * h + 3):
                lhs.append(side_by_side([all_parents[par_src_s[p, 0, i]] for i in range(4 * q, min(4 * q + 4, 27))]))
            term = dot(jnp.concatenate(lhs, axis=0), par_w[h, q])
            total = term if total is None else total + term
        sums += [total[32 * n:32 * n + 32, 64 * n:64 * n + 64] for n in range(3)]
    for p in range(PARENTS):
        total = sums[p] + top_down[:, 64 * p:64 * p + 64]
        field = leaf_acc[p] + dot_t(total.astype(BF16), lt_v[4 * p:4 * p + 4].reshape(256, 64))
        field = field.astype(BF16)
        masked = jnp.concatenate(
            [jnp.where(lane == c, field, jnp.zeros_like(field)) for c in range(4)], axis=0
        )
        far = dot(masked, basis_v[4 * p:4 * p + 4].reshape(256, 256))
        for c in range(4):
            g = 4 * p + c
            out_v[:, g * PTS:(g + 1) * PTS] = (near_acc[g] + far[32 * c:32 * c + 32]).astype(BF16)
        columns = pl.ds(4 * p * PTS, 4 * PTS)
        pltpu.make_async_copy(out_v.at[:, columns], out.at[:, columns], out_sem).start()

    await_tiles(spread_send, 3 * 7)
    await_tiles(across_send, 12 * 7)
    await_tiles(onward_send, 32 * 7)
    await_tiles(opposite_send, 16 * 7)
    await_tiles(share_send, 64 * 7)
    pltpu.make_async_copy(out_v, out_v, out_sem).wait()


def local(
    right_sides, near_blocks, near_cols, near_count, basis, leaf_transfer, par_transfer,
    leaf_src, leaf_coup, par_src, par_coup, top_src, top_coup,
):
    vma = pltpu.VMEM
    call = pl.pallas_call(
        kernel,
        out_shape=jax.ShapeDtypeStruct((32, LEAVES * PTS), BF16),
        in_specs=[pl.BlockSpec(memory_space=pl.ANY)] * 13,
        out_specs=pl.BlockSpec(memory_space=pl.ANY),
        scratch_shapes=[
            vma((LEAVES + 1, 32, PTS), BF16),
            vma((ZERO + 1, 32, PTS), BF16),
            vma((LEAVES, NEAR, PTS, PTS), BF16),
            vma((LEAVES, 64, PTS), BF16),
            vma((LEAVES, 64, 64), BF16),
            vma((PARENTS, 64, 64), BF16),
            vma((LEAVES, 8, 64, 64), BF16),
            vma((PARENTS, 27, 64, 64), BF16),
            vma((27, 64, 64), BF16),
            vma((32, LEAVES * PTS), BF16),
            pltpu.SMEM((NEAR, 1, LEAVES), jnp.int32),
            pltpu.SMEM((1, LEAVES), jnp.int32),
            pltpu.SMEM((8, LEAVES), jnp.int32),
            pltpu.SMEM((PARENTS, 1, 27), jnp.int32),
            pltpu.SMEM((1, 1, 27), jnp.int32),
            vma((LEAVES + 2 * HALO, 16, 128), BF16),
            vma((4, 2, 4, 4, PARENTS, 16, 128), BF16),
            vma((2, 4, 4, 4, 16, 128), BF16),
            vma((2, QUADS, 256, 256), BF16),
            vma((LEAVES, 32, PTS), F32),
            vma((PARENTS, 32, PTS), F32),
            pltpu.SemaphoreType.DMA,
            pltpu.SemaphoreType.DMA((12,)),
            pltpu.SemaphoreType.DMA((LEAVES // 2,)),
            pltpu.SemaphoreType.DMA((2,)),
            pltpu.SemaphoreType.DMA((2,)),
            pltpu.SemaphoreType.DMA,
            pltpu.SemaphoreType.DMA,
            pltpu.SemaphoreType.DMA((4,)),
            pltpu.SemaphoreType.DMA,
            pltpu.SemaphoreType.DMA((12,)),
            pltpu.SemaphoreType.DMA,
            pltpu.SemaphoreType.DMA((4,)),
            pltpu.SemaphoreType.DMA,
            pltpu.SemaphoreType.DMA((4,)),
            pltpu.SemaphoreType.DMA,
            pltpu.SemaphoreType.DMA((2,)),
            pltpu.SemaphoreType.DMA,
        ],
        compiler_params=pltpu.CompilerParams(
            collective_id=0, has_side_effects=True, vmem_limit_bytes=63 * 2**20
        ),
    )
    out = call(
        right_sides[:, 0],
        near_blocks[0],
        jnp.transpose(near_cols, (2, 0, 1)),
        near_count,
        jnp.swapaxes(basis[0], 1, 2),
        leaf_transfer[0],
        par_transfer[0],
        jnp.transpose(leaf_src[0], (1, 0)),
        leaf_coup[0],
        jnp.transpose(par_src, (1, 0, 2)),
        par_coup[0],
        top_src,
        top_coup[0, 0],
    )
    return out[:, None, :]


def solution(mesh):
    return jax.shard_map(
        local,
        mesh=mesh,
        in_specs=(
            P(None, "leaf", "clus"),
            P("leaf", "clus", None, None, None),
            P("leaf", "clus", None),
            P("leaf", "clus"),
            P("leaf", "clus", None, None),
            P("leaf", "clus", None, None),
            P("leaf", "clus", None, None),
            P("leaf", "clus", None),
            P("leaf", "clus", None, None, None),
            P("leaf", "clus", None),
            P("leaf", "clus", None, None, None),
            P("leaf", "clus", None),
            P("leaf", "clus", None, None, None),
        ),
        out_specs=P(None, "leaf", "clus"),
        check_vma=False,
    )
```
